128 devices in a mesh: seq: 16 (over y, z), head: 8 (over x, core).
Axes of the slice: x: 4, y: 4, z: 4, core: 2. Of those that a mesh axis runs over, the one named last changes fastest.
Arguments:
- tokens: bfloat16 [4, 16384, 8192], P(None, 'seq', 'head'), may hold values from -60 to 60
- state_inputs: bfloat16 [4, 16384, 1024], P(None, 'seq', 'head'), may hold values from -4 to 4
- state_reads: bfloat16 [4, 16384, 1024], P(None, 'seq', 'head'), may hold values from -2.1213203 to 2.1213203
- log_decay: float32 [4, 128, 16384], P(None, 'head', 'seq'), may hold values from -1 to 0
- norm_gain: float32 [8192], P('head'), may hold values from 0.5 to 1.5
- probe_tokens: bfloat16 [96, 64, 8192], P('seq', None, 'head'), may hold values from -60 to 60
- probe_inputs: bfloat16 [96, 64, 1024], P('seq', None, 'head'), may hold values from -4 to 4
- probe_reads: bfloat16 [96, 64, 1024], P('seq', None, 'head'), may hold values from -2.1213203 to 2.1213203
- probe_decay: float32 [96, 128, 64], P('seq', 'head'), may hold values from -1 to 0
- branch_premise: int32 [96], replicated, may hold values from 0 to 3
- branch_position: int32 [96], replicated, may hold values from 0 to 16383, as said below
Outputs:
- premise_out: bfloat16 [4, 16384, 8192], P(None, 'seq', 'head')
- probe_out: bfloat16 [96, 64, 8192], P('seq', None, 'head')
The draws below stay inside these ranges and needn't reach their ends.
Inputs may be any that keep to these rules, and one draw needn't show every extreme that they name: `branch_position`: probes g * 6 to g * 6 + 5 branch at positions whose values of position // 1024 are all different.
All inputs are finite; a program needn't handle non-finite values.
Results may differ from the reference program's by a relative error of at most 0.0046.
Values may be sent and summed in bfloat16 or wider, within the bound.
No kernel may reach another device: no remote copies, remote signals or barrier semaphores. Data moves between devices by JAX's collectives and lax.ppermute only.
A program may use at most 256 MiB of HBM per device.

```python
import math
import jax
import jax.numpy as jnp
from jax import lax

HEAD_TOTAL = 128
HEADDIM = 64
DSTATE = 128
GROUPS = 8
DIN = 8192
SPAN = 256
PREMISES = 4
SEQ_DEV = 1024
PLEN = 64
PROBE_DEV = 6
SEQLEN = 16384
PROBES = 96


def head_rates(key):
    key_pick, key_slow, key_fast = jax.random.split(jax.random.fold_in(key, 101), 3)
    slow_share = 0.5
    slow_heads = jax.random.uniform(key_pick, (HEAD_TOTAL,)) < slow_share
    slow_rate = jnp.exp(jax.random.uniform(key_slow, (HEAD_TOTAL,), minval=math.log(0.08), maxval=math.log(0.8))) / SEQLEN
    fast_rate = jnp.exp(jax.random.uniform(key_fast, (HEAD_TOTAL,), minval=math.log(1.0 / 50.0), maxval=math.log(1.0 / 30.0)))
    return jnp.where(slow_heads, slow_rate, fast_rate)


def decay_matrix_rows(key, front_part, total_length, with_spikes, random_seed):
    rates = head_rates(key)
    key_factor, key_locations, key_strength = jax.random.split(jax.random.fold_in(key, random_seed), 3)
    factor = jax.random.uniform(key_factor, (front_part, HEAD_TOTAL, total_length), minval=0.5, maxval=1.5)
    final_result = rates[None, :, None] * factor
    if with_spikes:
        spike_locations = jax.random.randint(key_locations, (front_part, 2), 0, total_length)
        marked_hits = jnp.any(jnp.arange(total_length)[None, None, :] == spike_locations[:, :, None], axis=1)
        spike_depth = jax.random.uniform(key_strength, (front_part, HEAD_TOTAL, total_length), minval=0.22, maxval=0.69)
        final_result = final_result + jnp.where(marked_hits[:, None, :], spike_depth, 0.0)
    return -final_result


def token_law(key, dims_shape, random_seed):
    key_base, key_rows, key_cols = jax.random.split(jax.random.fold_in(key, random_seed), 3)
    base_draw = jnp.clip(jax.random.normal(key_base, dims_shape), -4.0, 4.0)
    col_low = 0.3
    col_high = 3.0
    row_scale = jnp.exp(jax.random.uniform(key_rows, dims_shape[:-1] + (1,), minval=math.log(0.3), maxval=math.log(3.0)))
    col_scale = jnp.exp(jax.random.uniform(key_cols, (dims_shape[-1],), minval=math.log(col_low), maxval=math.log(col_high)))
    return base_draw * row_scale * col_scale


def group_scales(key):
    scale_low = 1.0
    scale_high = 4.0
    return jnp.exp(jax.random.uniform(jax.random.fold_in(key, 202), (GROUPS,), minval=math.log(scale_low), maxval=math.log(scale_high)))


def read_law(key, front_part, total_length, random_seed):
    scales = group_scales(key)
    key_base = jax.random.fold_in(key, random_seed)
    raw_draw = jnp.clip(jax.random.normal(key_base, (front_part, total_length, GROUPS, DSTATE)), -4.0, 4.0)
    return (raw_draw * scales[:, None] / math.sqrt(DSTATE)).reshape(front_part, total_length, GROUPS * DSTATE)


def draw_tokens(key, part):
    return token_law(key, (PREMISES, SEQLEN, DIN), 31).astype(jnp.bfloat16)


def draw_probe_tokens(key, part):
    return token_law(key, (PROBES, PLEN, DIN), 32).astype(jnp.bfloat16)


def draw_state_reads(key, part):
    return read_law(key, PREMISES, SEQLEN, 41).astype(jnp.bfloat16)


def draw_probe_reads(key, part):
    return read_law(key, PROBES, PLEN, 42).astype(jnp.bfloat16)


def draw_log_decay(key, part):
    return decay_matrix_rows(key, PREMISES, SEQLEN, True, 7)


def draw_probe_decay(key, part):
    return decay_matrix_rows(key, PROBES, PLEN, False, 8)


def draw_branch_position(key, part):
    key_heat, key_rating, key_offset = jax.random.split(jax.random.fold_in(key, 17), 3)
    possessor_count = SEQLEN // SEQ_DEV
    keeper_count = PROBES // PROBE_DEV
    warmth_level = jax.random.randint(key_heat, (possessor_count,), 0, 4)
    extra_score = jnp.where(warmth_level == 0, 4000, 0)
    score_values = jax.random.randint(key_rating, (keeper_count, possessor_count), 0, 1000) + extra_score[None, :]
    score_values = score_values * possessor_count + jnp.arange(possessor_count, dtype=jnp.int32)[None, :]
    _, picks = lax.top_k(score_values, PROBE_DEV)
    offsets = jax.random.randint(key_offset, (keeper_count, PROBE_DEV), 0, SEQ_DEV)
    return (picks * SEQ_DEV + offsets).reshape(PROBES).astype(jnp.int32)


def set_ends(array, key, least, largest):
    dims = array.shape
    place = [jax.random.randint(jax.random.fold_in(key, axis), (), 0, dims[axis]) for axis in range(len(dims))]
    array = array.at[tuple(place)].set(least)
    longest = dims.index(max(dims))
    place[longest] = (place[longest] + 1) % dims[longest]
    return array.at[tuple(place)].set(largest)


def levels(stream_key, shape, pieces, smallest, high):
    loudness, own = 1.0, jax.random.fold_in(stream_key, 6)
    for axis_at, blocks in pieces:
        heights = jnp.exp(jax.random.uniform(jax.random.fold_in(own, axis_at), (blocks,), jnp.float32, smallest / len(pieces), high / len(pieces)))
        loudness = loudness * jnp.repeat(heights, shape[axis_at] // blocks).reshape([-1 if axis == axis_at else 1 for axis in range(len(shape))])
    return loudness


def normal_values(rng, dims, scale, reach, pieces=(), kind=jnp.bfloat16):
    array = jax.random.normal(rng, dims, jnp.float32) * scale
    if len(pieces) > 0:
        array = levels(rng, dims, pieces, -0.22, 0.18) * array
    return jnp.clip(array, min=-reach, max=reach).astype(kind)


def setup_inputs(seed: int = 0) -> dict:
    arg_keys = jax.random.split(jax.random.key(seed), 12)
    tokens = draw_tokens(jax.random.fold_in(arg_keys[11], 71), 0)
    state_inputs = normal_values(arg_keys[1], (PREMISES, SEQLEN, GROUPS * DSTATE), 1.0, 4.0, ((1, 16), (2, 8)))
    state_reads = draw_state_reads(jax.random.fold_in(arg_keys[11], 71), 0)
    log_decay = draw_log_decay(jax.random.fold_in(arg_keys[11], 71), 0)
    norm_gain = jnp.clip(1.0 + 0.1 * jax.random.normal(arg_keys[4], (DIN,), jnp.float32), 0.5, 1.5)
    probe_tokens = draw_probe_tokens(jax.random.fold_in(arg_keys[11], 71), 0)
    probe_inputs = normal_values(arg_keys[6], (PROBES, PLEN, GROUPS * DSTATE), 1.0, 4.0, ((0, 16), (2, 8)))
    probe_reads = draw_probe_reads(jax.random.fold_in(arg_keys[11], 71), 0)
    probe_decay = draw_probe_decay(jax.random.fold_in(arg_keys[11], 71), 0)
    branch_premise = set_ends(jax.random.randint(arg_keys[9], (PROBES,), 0, PREMISES), jax.random.fold_in(arg_keys[9], 1), 0, PREMISES - 1).astype(jnp.int32)
    branch_position = draw_branch_position(jax.random.fold_in(arg_keys[11], 71), 0)
    return dict(tokens=tokens, state_inputs=state_inputs, state_reads=state_reads, log_decay=log_decay, norm_gain=norm_gain, probe_tokens=probe_tokens, probe_inputs=probe_inputs, probe_reads=probe_reads, probe_decay=probe_decay, branch_premise=branch_premise, branch_position=branch_position)


PRECISE = lax.Precision.HIGHEST
EPSILON = 1e-05

def rounded(values):
    return lax.optimization_barrier(values.astype(jnp.bfloat16)).astype(jnp.float32)

def block_parts(block_x, block_in, block_read, block_decay):
    block_len = block_x.shape[0]
    per_group = HEAD_TOTAL // GROUPS
    values = block_x.astype(jnp.float32).reshape(block_len, GROUPS, per_group, HEADDIM)
    inputs = block_in.astype(jnp.float32).reshape(block_len, GROUPS, DSTATE)
    read_rows = block_read.astype(jnp.float32).reshape(block_len, GROUPS, DSTATE)
    cumulative = jnp.cumsum(block_decay, axis=1).reshape(GROUPS, per_group, block_len)
    gram_block = jnp.einsum('tgn,ugn->gtu', read_rows, inputs, precision=PRECISE)
    causal = jnp.arange(block_len)[:, None] >= jnp.arange(block_len)[None, :]
    spread = cumulative[..., :, None] - cumulative[..., None, :]
    weights = rounded(jnp.where(causal, jnp.exp(jnp.where(causal, spread, 0.0)), 0.0) * gram_block[:, None])
    inner_part = jnp.einsum('ghtu,ughp->tghp', weights, values, precision=PRECISE)
    tail_decay = jnp.exp(cumulative[..., -1:] - cumulative)
    scaled = rounded(values * jnp.transpose(tail_decay, (2, 0, 1))[..., None])
    written = jnp.einsum('tghp,tgn->ghpn', scaled, inputs, precision=PRECISE)
    return (inner_part, written, cumulative, read_rows)

def normalize(mixed, norm_gain):
    flat_rows = mixed.reshape(mixed.shape[0], DIN)
    square_sum = lax.optimization_barrier(jnp.sum(flat_rows * flat_rows, axis=-1, keepdims=True))
    return (flat_rows * lax.rsqrt(square_sum / DIN + EPSILON) * norm_gain).astype(jnp.bfloat16)

def run_sequence(seq_x, seq_in, seq_read, seq_decay, block_len, start_state, norm_gain):
    block_count = seq_x.shape[0] // block_len

    def advance(carried, block_index):
        start_row = block_index * block_len
        block_x = lax.dynamic_slice_in_dim(seq_x, start_row, block_len, 0)
        block_in = lax.dynamic_slice_in_dim(seq_in, start_row, block_len, 0)
        block_read = lax.dynamic_slice_in_dim(seq_read, start_row, block_len, 0)
        block_decay = lax.dynamic_slice_in_dim(seq_decay, start_row, block_len, 1)
        inner_part, written, cumulative, read_rows = block_parts(block_x, block_in, block_read, block_decay)
        applied = jnp.einsum('tgn,ghpn->tghp', read_rows, carried, precision=PRECISE)
        mixed = inner_part + jnp.exp(jnp.transpose(cumulative, (2, 0, 1)))[..., None] * applied
        next_state = jnp.exp(cumulative[..., -1])[..., None, None] * carried + written
        return (next_state, (normalize(mixed, norm_gain), carried))
    _, (outputs, starts) = lax.scan(advance, start_state, jnp.arange(block_count, dtype=jnp.int32))
    return (outputs.reshape(seq_x.shape[0], DIN), starts)

def reference(tokens, state_inputs, state_reads, log_decay, norm_gain, probe_tokens, probe_inputs, probe_reads, probe_decay, branch_premise, branch_position):
    per_group = HEAD_TOTAL // GROUPS
    zero_state = jnp.zeros((GROUPS, per_group, HEADDIM, DSTATE), jnp.float32)
    premise_rows = []
    premise_starts = []
    for premise in range(PREMISES):
        outputs, starts = run_sequence(tokens[premise], state_inputs[premise], state_reads[premise], log_decay[premise], SPAN, zero_state, norm_gain)
        premise_rows.append(outputs)
        premise_starts.append(starts)
    premise_out = jnp.stack(premise_rows)
    all_starts = jnp.stack(premise_starts)
    zero_index = jnp.zeros((), jnp.int32)

    def one_probe(probe_index):
        premise = branch_premise[probe_index].astype(jnp.int32)
        position = branch_position[probe_index].astype(jnp.int32)
        block_idx = (position // SPAN).astype(jnp.int32)
        within = (position % SPAN).astype(jnp.int32)
        start_state = all_starts[premise, block_idx]
        start_row = (block_idx * SPAN).astype(jnp.int32)
        block_x = lax.dynamic_slice(tokens, (premise, start_row, zero_index), (1, SPAN, DIN))[0]
        block_in = lax.dynamic_slice(state_inputs, (premise, start_row, zero_index), (1, SPAN, GROUPS * DSTATE))[0]
        block_decay = lax.dynamic_slice(log_decay, (premise, zero_index, start_row), (1, HEAD_TOTAL, SPAN))[0]
        values = block_x.astype(jnp.float32).reshape(SPAN, GROUPS, per_group, HEADDIM)
        inputs = block_in.astype(jnp.float32).reshape(SPAN, GROUPS, DSTATE)
        cumulative = jnp.cumsum(block_decay, axis=1).reshape(GROUPS, per_group, SPAN)
        here_cum = lax.dynamic_index_in_dim(cumulative, within, axis=2, keepdims=False)
        keep_mask = jnp.arange(SPAN) <= within
        weights = jnp.where(keep_mask, jnp.exp(jnp.where(keep_mask, here_cum[..., None] - cumulative, 0.0)), 0.0)
        scaled = rounded(values * jnp.transpose(weights, (2, 0, 1))[..., None])
        fresh_part = jnp.einsum('tghp,tgn->ghpn', scaled, inputs, precision=PRECISE)
        branch = jnp.exp(here_cum)[..., None, None] * start_state + fresh_part
        outputs, _ = run_sequence(probe_tokens[probe_index], probe_inputs[probe_index], probe_reads[probe_index], probe_decay[probe_index], min(PLEN, SPAN), branch, norm_gain)
        return outputs
    probe_out = lax.map(one_probe, jnp.arange(PROBES, dtype=jnp.int32))
    return (premise_out, probe_out)
```

```python
import functools

import jax
import jax.numpy as jnp
from jax import lax
from jax.experimental import pallas as pl
from jax.experimental.pallas import tpu as pltpu
from jax.sharding import PartitionSpec as P

F32 = jnp.float32
BF16 = jnp.bfloat16
DSTATE = 128
DIN = 8192
EPSILON = 1e-05
BLOCK = 128
EXTRA = 16


def dot(left, right, left_dim, right_dim, precision=None):
    return lax.dot_general(
        left,
        right,
        (((left_dim,), (right_dim,)), ((), ())),
        precision=precision,
        preferred_element_type=F32,
    )


def pieces(value, count):
    parts = []
    for _ in range(count):
        part = value.astype(BF16)
        parts.append(part)
        value = value - part.astype(F32)
    return parts


def spread(heads, width):
    shape = (heads, width)
    head = lax.broadcasted_iota(jnp.int32, shape, 0)
    channel = lax.broadcasted_iota(jnp.int32, shape, 1)
    per_head = width // heads
    return jnp.where(lax.div(channel, jnp.int32(per_head)) == head, 1.0, 0.0).astype(F32)


def spread_twice(one):
    half = one.astype(BF16)
    return jnp.concatenate([half, half], axis=0)


def widen(value, twice):
    return dot(jnp.concatenate(pieces(value, 2), axis=0), twice, 0, 0)


def widen_column(column, one):
    return jnp.sum(column * one, axis=0, keepdims=True)


def prefix(decay, length):
    heads = decay.shape[0]
    count = decay.shape[1] // length
    parts = pieces(decay, 3)
    rows = [part[:, k * length : (k + 1) * length] for k in range(count) for part in parts]
    shape = (length, length)
    upto = (
        lax.broadcasted_iota(jnp.int32, shape, 0) <= lax.broadcasted_iota(jnp.int32, shape, 1)
    )
    total = dot(jnp.concatenate(rows, axis=0), jnp.where(upto, 1.0, 0.0).astype(BF16), 1, 0)
    out = []
    for k in range(count):
        base = 3 * heads * k
        out.append(
            total[base : base + heads]
            + total[base + heads : base + 2 * heads]
            + total[base + 2 * heads : base + 3 * heads]
        )
    return out


def causal(queries, keys):
    shape = (queries, keys)
    return lax.broadcasted_iota(jnp.int32, shape, 0) >= lax.broadcasted_iota(jnp.int32, shape, 1)


def route_kernel(position_ref, me_ref, reads_ref, decay_ref, out_ref, *, seq_dev):
    slots = out_ref.shape[0]
    probe_dev, probe_len, _ = reads_ref.shape
    rows, heads, length = decay_ref.shape
    decay = decay_ref[...].reshape(rows * heads, length)
    ones = jnp.ones((EXTRA, length), BF16)
    fill = jnp.zeros((DSTATE - rows * heads, length), BF16)
    total = 0.0
    for part in pieces(decay, 3):
        total = total + dot(ones, jnp.concatenate([part, fill], axis=0), 1, 1)
    row = lax.broadcasted_iota(jnp.int32, (EXTRA, DSTATE), 0)
    block = jnp.zeros((EXTRA, DSTATE), F32)
    for index, part in enumerate(pieces(total, 3)):
        block = jnp.where(row == index, part.astype(F32), block)
    block = block.astype(BF16)
    nothing = jnp.zeros((probe_len, DSTATE), BF16)
    for slot in range(slots):
        out_ref[slot, 0:probe_len, :] = nothing
        out_ref[slot, probe_len : probe_len + EXTRA, :] = block
    for probe in range(probe_dev):
        owner = lax.div(position_ref[me_ref[0] * probe_dev + probe], jnp.int32(seq_dev))
        out_ref[owner, 0:probe_len, :] = reads_ref[probe]


def end_kernel(x_ref, in_ref, decay_ref, out_ref, scaled_ref):
    _, length, width = x_ref.shape
    heads = decay_ref.shape[1]
    twice = spread_twice(spread(heads, width))
    sums = prefix(decay_ref[0], BLOCK)
    after = jnp.zeros((heads, 1), F32)
    for k in reversed(range(length // BLOCK)):
        rows = slice(k * BLOCK, (k + 1) * BLOCK)
        last = sums[k][:, BLOCK - 1 : BLOCK]
        factor = widen(jnp.exp((last - sums[k]) + after), twice)
        scaled_ref[rows, :] = (x_ref[0, rows, :].astype(F32) * factor).astype(BF16)
        after = after + last
    out_ref[0] = dot(in_ref[0], scaled_ref[...], 0, 0).astype(BF16)


def find_slot(slot, position_ref, premise_ref, me, probe_dev, seq_dev):
    offset = jnp.int32(0)
    premise = jnp.int32(0)
    present = jnp.int32(0)
    for probe in range(probe_dev):
        position = position_ref[slot * probe_dev + probe]
        here = lax.div(position, jnp.int32(seq_dev)) == me
        offset = jnp.where(here, position - me * seq_dev, offset)
        premise = jnp.where(here, premise_ref[slot * probe_dev + probe], premise)
        present = jnp.where(here, jnp.int32(1), present)
    return offset, premise, present


def chain_factors(sums, one):
    middle = BLOCK // 2 - 1
    factors = []
    tail = None
    for k in range(len(sums)):
        mid = sums[k][:, middle : middle + 1]
        step = mid if tail is None else tail + mid
        factors.append(widen_column(jnp.exp(step), one))
        tail = sums[k][:, BLOCK - 1 : BLOCK] - mid
    return factors


def branch_kernel(
    position_ref,
    premise_ref,
    me_ref,
    x_ref,
    in_ref,
    decay_ref,
    routed_ref,
    out_ref,
    scale_ref,
    right_ref,
    state_ref,
    near_ref,
    far_ref,
    *,
    seq_dev,
    probe_dev,
):
    _, length, width = x_ref.shape
    heads = decay_ref.shape[1]
    slots, probe_len, _ = out_ref.shape
    row = pl.program_id(0)
    middle = BLOCK // 2 - 1

    @pl.when(row == 0)
    def _():
        out_ref[...] = jnp.zeros_like(out_ref)
        scale_ref[...] = jnp.zeros_like(scale_ref)

    one = spread(heads, width)
    twice = spread_twice(one)
    sums = prefix(decay_ref[0], BLOCK)
    factors = chain_factors(sums, one)
    before = jnp.zeros((heads, 1), F32)
    state_ref[...] = jnp.zeros_like(state_ref)
    for k in range(length // BLOCK):
        rows = slice(k * BLOCK, (k + 1) * BLOCK)
        near = sums[k] - sums[k][:, middle : middle + 1]
        near_ref[k] = near
        far_ref[k] = sums[k] + before
        before = before + sums[k][:, BLOCK - 1 : BLOCK]
        scaled = (x_ref[0, rows, :].astype(F32) * widen(jnp.exp(-near), twice)).astype(BF16)
        right_ref[k, 0:BLOCK, :] = scaled
        state = state_ref[...] * factors[k]
        right_ref[k, BLOCK : BLOCK + DSTATE, :] = state.astype(BF16)
        state_ref[...] = state + dot(in_ref[0, rows, :], scaled, 0, 0)

    def one_slot(slot, carry):
        offset, premise, present = find_slot(
            slot, position_ref, premise_ref, me_ref[0], probe_dev, seq_dev
        )

        @pl.when((present == 1) & (premise == row))
        def _():
            k = lax.div(offset, jnp.int32(BLOCK))
            within = offset - k * BLOCK
            reads = routed_ref[slot, 0:probe_len, :]
            inputs = in_ref[0, pl.ds(pl.multiple_of(k * BLOCK, BLOCK), BLOCK), :]
            keep = lax.broadcasted_iota(jnp.int32, (probe_len, BLOCK), 1) <= within
            gram = jnp.where(keep, dot(reads, inputs, 1, 1), 0.0).astype(BF16)
            product = dot(jnp.concatenate([gram, reads], axis=1), right_ref[k], 1, 0)
            here = lax.broadcasted_iota(jnp.int32, (heads, BLOCK), 1) == within

            def at(ref):
                value = jnp.sum(jnp.where(here, ref[k], 0.0), axis=1, keepdims=True)
                return widen_column(jnp.exp(value), one)

            out_ref[slot] = product * at(near_ref)
            scale_ref[slot] = jnp.broadcast_to(at(far_ref), (8, width))

        return carry

    lax.fori_loop(0, slots, one_slot, 0)


def scan_kernel(me_ref, part_ref, routed_ref, out_ref, *, probe_len, heads, rows):
    count, height, width = part_ref.shape
    premise = lax.div(me_ref[0] * height, jnp.int32(DSTATE))
    shape = (DSTATE, width)
    lane = lax.broadcasted_iota(jnp.int32, shape, 0) - premise * heads
    channel = lax.broadcasted_iota(jnp.int32, shape, 1)
    pick = jnp.where(lax.div(channel, jnp.int32(width // heads)) == lane, 1.0, 0.0).astype(BF16)
    state = jnp.zeros((height, width), F32)
    for k in range(count):
        out_ref[k] = state.astype(BF16)
        total = dot(routed_ref[k, probe_len : probe_len + EXTRA, :], pick, 1, 0)
        total = jnp.sum(total[0:8], axis=0, keepdims=True)
        state = state * jnp.exp(total) + part_ref[k].astype(F32)


def apply_kernel(
    position_ref,
    premise_ref,
    me_ref,
    incoming_ref,
    routed_ref,
    local_ref,
    scale_ref,
    out_ref,
    *,
    seq_dev,
    probe_dev,
):
    step, probe_len, _ = out_ref.shape
    for index in range(step):
        slot = pl.program_id(0) * step + index
        _, premise, _ = find_slot(slot, position_ref, premise_ref, me_ref[0], probe_dev, seq_dev)
        product = dot(routed_ref[index, 0:probe_len, :], incoming_ref[premise], 1, 0)
        out_ref[index] = (product * scale_ref[index, 0:1, :] + local_ref[index]).astype(BF16)


def squares(mixed):
    total = mixed[:, 0:128] * mixed[:, 0:128]
    for k in range(1, mixed.shape[1] // 128):
        part = mixed[:, 128 * k : 128 * (k + 1)]
        total = total + part * part
    return dot(jnp.ones((8, 128), F32), total, 1, 1, lax.Precision.HIGHEST)


def main_kernel(
    x_ref, in_ref, read_ref, decay_ref, incoming_ref, out_ref, square_ref, right_ref, state_ref
):
    _, length, width = x_ref.shape
    heads = decay_ref.shape[1]
    middle = BLOCK // 2 - 1
    one = spread(heads, width)
    twice = spread_twice(one)
    sums = prefix(decay_ref[0], BLOCK)
    factors = chain_factors(sums, one)
    mask = causal(BLOCK, BLOCK)
    line = lax.broadcasted_iota(jnp.int32, (8, BLOCK), 0)
    total = jnp.zeros((8, BLOCK), F32)
    state_ref[...] = incoming_ref[0].astype(F32)
    for k in range(length // BLOCK):
        rows = slice(k * BLOCK, (k + 1) * BLOCK)
        near = sums[k] - sums[k][:, middle : middle + 1]
        inputs = in_ref[0, rows, :]
        reads = read_ref[0, rows, :]
        scaled = (x_ref[0, rows, :].astype(F32) * widen(jnp.exp(-near), twice)).astype(BF16)
        right = right_ref.at[k % 2]
        right[0:BLOCK, :] = scaled
        state = state_ref[...] * factors[k]
        right[BLOCK : BLOCK + DSTATE, :] = state.astype(BF16)
        state_ref[...] = state + dot(inputs, scaled, 0, 0)
        gram = jnp.where(mask, dot(reads, inputs, 1, 1), 0.0).astype(BF16)
        product = dot(jnp.concatenate([gram, reads], axis=1), right[...], 1, 0)
        mixed = product * widen(jnp.exp(near), twice)
        out_ref[0, rows, :] = mixed
        total = jnp.where(line == k, squares(mixed), total)
    for copy in range(square_ref.shape[0]):
        square_ref[copy, 0] = total


def probe_kernel(
    position_ref,
    me_ref,
    x_ref,
    in_ref,
    read_ref,
    decay_ref,
    arrived_ref,
    out_ref,
    square_ref,
    *,
    seq_dev,
):
    probe_dev, length, width = x_ref.shape
    heads = decay_ref.shape[1]
    twice = spread_twice(spread(heads, width))
    mask = causal(length, length)
    line = lax.broadcasted_iota(jnp.int32, (8, 128), 0)
    total = jnp.zeros((8, 128), F32)
    pair = 128 // length
    for probe in range(probe_dev):
        owner = lax.div(position_ref[me_ref[0] * probe_dev + probe], jnp.int32(seq_dev))
        sums = prefix(decay_ref[probe], length)[0]
        inputs = in_ref[probe]
        scaled = (x_ref[probe].astype(F32) * widen(jnp.exp(-sums), twice)).astype(BF16)
        gram = jnp.where(mask, dot(read_ref[probe], inputs, 1, 1), 0.0).astype(BF16)
        product = dot(gram, scaled, 1, 0) + arrived_ref[owner].astype(F32)
        out_ref[0, probe * length : (probe + 1) * length, :] = product * widen(
            jnp.exp(sums), twice
        )
    for k in range(probe_dev // pair):
        total = jnp.where(line == k, squares(out_ref[0, 128 * k : 128 * (k + 1), :]), total)
    for copy in range(square_ref.shape[0]):
        square_ref[copy, 0] = total


def norm_kernel(mixed_ref, square_ref, gain_ref, out_ref):
    _, length, width = mixed_ref.shape
    total = jnp.sum(square_ref[:, 0], axis=0)
    rate = lax.rsqrt(total / DIN + EPSILON)
    high, low = (part.astype(F32) for part in pieces(rate, 2))
    left = jnp.concatenate([high, low, high, low], axis=0).astype(BF16)
    gain = gain_ref[...]
    gain_high, gain_low = (part.astype(F32) for part in pieces(gain, 2))
    shape = (32, width)
    line = lax.broadcasted_iota(jnp.int32, shape, 0)
    both = jnp.where(
        line < 16, jnp.broadcast_to(gain_high, shape), jnp.broadcast_to(gain_low, shape)
    )
    for k in range(length // 128):
        rows = slice(128 * k, 128 * (k + 1))
        right = jnp.where(lax.rem(line, 8) == k, both, 0.0).astype(BF16)
        out_ref[0, rows, :] = (mixed_ref[0, rows, :] * dot(left, right, 0, 0)).astype(BF16)


SMEM = pl.BlockSpec(memory_space=pltpu.SMEM)


def whole(shape):
    return pl.BlockSpec(shape, lambda *_: (0,) * len(shape))


def along(shape, dim=0):
    return pl.BlockSpec(shape, lambda i: tuple(i if d == dim else 0 for d in range(len(shape))))


def call(kernel, name, grid, in_specs, out_specs, out_shape, scratch=(), flops=0, moved=0):
    return pl.pallas_call(
        kernel,
        name=name,
        grid=grid,
        in_specs=in_specs,
        out_specs=out_specs,
        out_shape=out_shape,
        scratch_shapes=list(scratch),
        compiler_params=pltpu.CompilerParams(vmem_limit_bytes=58 * 1024 * 1024),
        cost_estimate=pl.CostEstimate(flops=flops, bytes_accessed=moved, transcendentals=0),
    )


def shaped(shape, dtype):
    return jax.ShapeDtypeStruct(shape, dtype)


def exchange(value, axis):
    return lax.all_to_all(value, axis, split_axis=0, concat_axis=0, tiled=True)


def local(
    tokens,
    state_inputs,
    state_reads,
    log_decay,
    norm_gain,
    probe_tokens,
    probe_inputs,
    probe_reads,
    probe_decay,
    branch_premise,
    branch_position,
):
    seq = lax.axis_size("seq")
    ring = lax.axis_size("head")
    me = lax.axis_index("seq").astype(jnp.int32).reshape(1)
    row_count, seq_dev, width = tokens.shape
    heads = log_decay.shape[1]
    probe_dev, probe_len, _ = probe_tokens.shape
    height = row_count * DSTATE // seq
    routed_shape = (seq, probe_len + EXTRA, DSTATE)

    routed = call(
        functools.partial(route_kernel, seq_dev=seq_dev),
        "route",
        (1,),
        [SMEM, SMEM, whole(probe_reads.shape), whole(log_decay.shape)],
        whole(routed_shape),
        shaped(routed_shape, BF16),
        moved=800_000,
    )(branch_position, me, probe_reads, log_decay)
    routed = exchange(routed, "seq")

    x_spec = along((1, seq_dev, width))
    in_spec = along((1, seq_dev, DSTATE))
    decay_spec = along((1, heads, seq_dev))
    state_spec = along((1, DSTATE, width))
    ends = call(
        end_kernel,
        "ends",
        (row_count,),
        [x_spec, in_spec, decay_spec],
        state_spec,
        shaped((row_count, DSTATE, width), BF16),
        [pltpu.VMEM((seq_dev, width), BF16)],
        flops=4_000_000_000,
        moved=11_000_000,
    )(tokens, state_inputs, log_decay)
    parts = exchange(ends.reshape(seq, height, width), "seq")

    count = seq_dev // BLOCK
    local_part, scale = call(
        functools.partial(branch_kernel, seq_dev=seq_dev, probe_dev=probe_dev),
        "branch",
        (row_count,),
        [SMEM, SMEM, SMEM, x_spec, in_spec, decay_spec, whole(routed_shape)],
        [whole((seq, probe_len, width)), whole((seq, 8, width))],
        [shaped((seq, probe_len, width), F32), shaped((seq, 8, width), F32)],
        [
            pltpu.VMEM((count, BLOCK + DSTATE, width), BF16),
            pltpu.VMEM((DSTATE, width), F32),
            pltpu.VMEM((count, heads, BLOCK), F32),
            pltpu.VMEM((count, heads, BLOCK), F32),
        ],
        flops=10_000_000_000,
        moved=14_000_000,
    )(branch_position, branch_premise, me, tokens, state_inputs, log_decay, routed)

    starts = call(
        functools.partial(scan_kernel, probe_len=probe_len, heads=heads, rows=row_count),
        "scan",
        (1,),
        [SMEM, whole((seq, height, width)), whole(routed_shape)],
        whole((seq, height, width)),
        shaped((seq, height, width), BF16),
        flops=1_000_000_000,
        moved=2_500_000,
    )(me, parts, routed)
    incoming = exchange(starts, "seq").reshape(row_count, DSTATE, width)

    step = 4
    answers = call(
        functools.partial(apply_kernel, seq_dev=seq_dev, probe_dev=probe_dev),
        "apply",
        (seq // step,),
        [
            SMEM,
            SMEM,
            SMEM,
            whole((row_count, DSTATE, width)),
            along((step,) + routed_shape[1:]),
            along((step, probe_len, width)),
            along((step, 8, width)),
        ],
        along((step, probe_len, width)),
        shaped((seq, probe_len, width), BF16),
        flops=1_000_000_000,
        moved=8_000_000,
    )(branch_position, branch_premise, me, incoming, routed, local_part, scale)
    arrived = exchange(answers, "seq")

    mixed, square = call(
        main_kernel,
        "main",
        (row_count,),
        [x_spec, in_spec, in_spec, decay_spec, state_spec],
        [x_spec, along((ring, 1, 8, 128), 1)],
        [shaped(tokens.shape, F32), shaped((ring, row_count, 8, 128), F32)],
        [pltpu.VMEM((2, BLOCK + DSTATE, width), BF16), pltpu.VMEM((DSTATE, width), F32)],
        flops=12_000_000_000,
        moved=28_000_000,
    )(tokens, state_inputs, state_reads, log_decay, incoming)
    square = exchange(square, "head")
    gain = norm_gain.reshape(1, width)
    premise_out = call(
        norm_kernel,
        "norm",
        (row_count,),
        [x_spec, along((ring, 1, 8, 128), 1), whole((1, width))],
        x_spec,
        shaped(tokens.shape, BF16),
        flops=2_000_000_000,
        moved=25_000_000,
    )(mixed, square, gain)

    probe_rows = (1, probe_dev * probe_len, width)
    probe_mixed, probe_square = call(
        functools.partial(probe_kernel, seq_dev=seq_dev),
        "probes",
        (1,),
        [SMEM, SMEM]
        + [
            whole(part.shape)
            for part in (probe_tokens, probe_inputs, probe_reads, probe_decay, arrived)
        ],
        [whole(probe_rows), whole((ring, 1, 8, 128))],
        [shaped(probe_rows, F32), shaped((ring, 1, 8, 128), F32)],
        flops=1_000_000_000,
        moved=5_000_000,
    )(
        branch_position,
        me,
        probe_tokens,
        probe_inputs,
        probe_reads,
        probe_decay,
        arrived,
    )
    probe_square = exchange(probe_square, "head")
    probe_out = call(
        norm_kernel,
        "probe_norm",
        (1,),
        [whole(probe_rows), whole((ring, 1, 8, 128)), whole((1, width))],
        whole(probe_rows),
        shaped(probe_rows, BF16),
        flops=100_000_000,
        moved=2_000_000,
    )(probe_mixed, probe_square, gain)
    return (premise_out, probe_out.reshape(probe_dev, probe_len, width))


def solution(mesh):
    return jax.shard_map(
        local,
        mesh=mesh,
        in_specs=(
            P(None, "seq", "head"),
            P(None, "seq", "head"),
            P(None, "seq", "head"),
            P(None, "head", "seq"),
            P("head"),
            P("seq", None, "head"),
            P("seq", None, "head"),
            P("seq", None, "head"),
            P("seq", "head", None),
            P(),
            P(),
        ),
        out_specs=(P(None, "seq", "head"), P("seq", None, "head")),
        check_vma=False,
    )
```

```python
import functools

import jax
import jax.numpy as jnp
from jax import lax
from jax.experimental import pallas as pl
from jax.experimental.pallas import tpu as pltpu
from jax.sharding import PartitionSpec as P

F32 = jnp.float32
BF16 = jnp.bfloat16
DSTATE = 128
DIN = 8192
EPSILON = 1e-05
BLOCK = 128
EXTRA = 16


def dot(left, right, left_dim, right_dim, precision=None):
    return lax.dot_general(
        left,
        right,
        (((left_dim,), (right_dim,)), ((), ())),
        precision=precision,
        preferred_element_type=F32,
    )


def pieces(value, count):
    parts = []
    for _ in range(count):
        part = value.astype(BF16)
        parts.append(part)
        value = value - part.astype(F32)
    return parts


def spread(heads, width):
    shape = (heads, width)
    head = lax.broadcasted_iota(jnp.int32, shape, 0)
    channel = lax.broadcasted_iota(jnp.int32, shape, 1)
    per_head = width // heads
    return jnp.where(lax.div(channel, jnp.int32(per_head)) == head, 1.0, 0.0).astype(F32)


def spread_twice(one):
    half = one.astype(BF16)
    return jnp.concatenate([half, half], axis=0)


def widen(value, twice):
    return dot(jnp.concatenate(pieces(value, 2), axis=0), twice, 0, 0)


def widen_column(column, one):
    return jnp.sum(column * one, axis=0, keepdims=True)


def prefix(decay, length):
    heads = decay.shape[0]
    count = decay.shape[1] // length
    parts = pieces(decay, 3)
    rows = [part[:, k * length : (k + 1) * length] for k in range(count) for part in parts]
    shape = (length, length)
    upto = (
        lax.broadcasted_iota(jnp.int32, shape, 0) <= lax.broadcasted_iota(jnp.int32, shape, 1)
    )
    total = dot(jnp.concatenate(rows, axis=0), jnp.where(upto, 1.0, 0.0).astype(BF16), 1, 0)
    out = []
    for k in range(count):
        base = 3 * heads * k
        out.append(
            total[base : base + heads]
            + total[base + heads : base + 2 * heads]
            + total[base + 2 * heads : base + 3 * heads]
        )
    return out


def causal(queries, keys):
    shape = (queries, keys)
    return lax.broadcasted_iota(jnp.int32, shape, 0) >= lax.broadcasted_iota(jnp.int32, shape, 1)


def route_kernel(
    position_ref, premise_ref, me_ref, reads_ref, decay_ref, out_ref, table_ref, *, seq_dev
):
    slots = out_ref.shape[0]
    probe_dev, probe_len, _ = reads_ref.shape
    rows, heads, length = decay_ref.shape
    decay = decay_ref[...].reshape(rows * heads, length)
    ones = jnp.ones((EXTRA, length), BF16)
    fill = jnp.zeros((DSTATE - rows * heads, length), BF16)
    total = 0.0
    for part in pieces(decay, 3):
        total = total + dot(ones, jnp.concatenate([part, fill], axis=0), 1, 1)
    row = lax.broadcasted_iota(jnp.int32, (EXTRA, DSTATE), 0)
    block = jnp.zeros((EXTRA, DSTATE), F32)
    for index, part in enumerate(pieces(total, 3)):
        block = jnp.where(row == index, part.astype(F32), block)
    block = block.astype(BF16)
    nothing = jnp.zeros((probe_len, DSTATE), BF16)
    for slot in range(slots):
        out_ref[slot, 0:probe_len, :] = nothing
        out_ref[slot, probe_len : probe_len + EXTRA, :] = block
    for probe in range(probe_dev):
        owner = lax.div(position_ref[me_ref[0] * probe_dev + probe], jnp.int32(seq_dev))
        out_ref[owner, 0:probe_len, :] = reads_ref[probe]
    me = me_ref[0]
    for slot in range(slots):
        offset = jnp.int32(0)
        premise = jnp.int32(0)
        present = jnp.int32(0)
        for probe in range(probe_dev):
            position = position_ref[slot * probe_dev + probe]
            here = lax.div(position, jnp.int32(seq_dev)) == me
            offset = jnp.where(here, position - me * seq_dev, offset)
            premise = jnp.where(here, premise_ref[slot * probe_dev + probe], premise)
            present = jnp.where(here, jnp.int32(1), present)
        block = lax.div(offset, jnp.int32(BLOCK))
        table_ref[4 * slot] = present
        table_ref[4 * slot + 1] = premise
        table_ref[4 * slot + 2] = block
        table_ref[4 * slot + 3] = offset - block * BLOCK


def end_kernel(x_ref, in_ref, decay_ref, out_ref, scaled_ref):
    _, length, width = x_ref.shape
    heads = decay_ref.shape[1]
    twice = spread_twice(spread(heads, width))
    sums = prefix(decay_ref[0], BLOCK)
    after = jnp.zeros((heads, 1), F32)
    for k in reversed(range(length // BLOCK)):
        rows = slice(k * BLOCK, (k + 1) * BLOCK)
        last = sums[k][:, BLOCK - 1 : BLOCK]
        factor = widen(jnp.exp((last - sums[k]) + after), twice)
        scaled_ref[rows, :] = (x_ref[0, rows, :].astype(F32) * factor).astype(BF16)
        after = after + last
    out_ref[0] = dot(in_ref[0], scaled_ref[...], 0, 0).astype(BF16)


def chain_factors(sums, one):
    middle = BLOCK // 2 - 1
    factors = []
    tail = None
    for k in range(len(sums)):
        mid = sums[k][:, middle : middle + 1]
        step = mid if tail is None else tail + mid
        factors.append(widen_column(jnp.exp(step), one))
        tail = sums[k][:, BLOCK - 1 : BLOCK] - mid
    return factors


def build_kernel(x_ref, in_ref, decay_ref, out_ref, done_ref):
    _, length, width = x_ref.shape
    heads = decay_ref.shape[1]
    middle = BLOCK // 2 - 1
    one = spread(heads, width)
    twice = spread_twice(one)
    sums = prefix(decay_ref[0], BLOCK)
    factors = chain_factors(sums, one)
    count = length // BLOCK
    done_ref[...] = jnp.zeros_like(done_ref)
    for k in range(count):
        rows = slice(k * BLOCK, (k + 1) * BLOCK)
        near = sums[k] - sums[k][:, middle : middle + 1]
        factor = widen(jnp.exp(-near), twice)
        out_ref[0, k, 0:BLOCK, :] = (x_ref[0, rows, :].astype(F32) * factor).astype(BF16)
    out_ref[0, 0, BLOCK : BLOCK + DSTATE, :] = jnp.zeros((DSTATE, width), BF16)
    written = [
        dot(in_ref[0, k * BLOCK : (k + 1) * BLOCK, :], out_ref[0, k, 0:BLOCK, :], 0, 0)
        for k in range(count - 1)
    ]
    state = written[0]
    for k in range(1, count):
        state = state * factors[k]
        out_ref[0, k, BLOCK : BLOCK + DSTATE, :] = state.astype(BF16)
        if k < count - 1:
            state = state + written[k]


def branch_kernel(table_ref, right_ref, in_ref, decay_ref, routed_ref, out_ref, scale_ref):
    _, probe_len, width = out_ref.shape
    _, heads, length = decay_ref.shape
    slot = pl.program_id(0)
    present = table_ref[4 * slot] == 1

    @pl.when(present)
    def _():
        k = table_ref[4 * slot + 2]
        within = table_ref[4 * slot + 3]
        reads = routed_ref[0, 0:probe_len, :]
        keep = lax.broadcasted_iota(jnp.int32, (probe_len, BLOCK), 1) <= within
        gram = jnp.where(keep, dot(reads, in_ref[0], 1, 1), 0.0).astype(BF16)
        product = dot(jnp.concatenate([gram, reads], axis=1), right_ref[0, 0], 1, 0)
        one = spread(heads, width)
        lane = lax.broadcasted_iota(jnp.int32, (heads, length), 1)
        offset = k * BLOCK + within
        middle = k * BLOCK + BLOCK // 2 - 1
        decay = decay_ref[0]
        far = jnp.sum(jnp.where(lane <= offset, decay, 0.0), axis=1, keepdims=True)
        later = jnp.where((lane > middle) & (lane <= offset), decay, 0.0)
        earlier = jnp.where((lane > offset) & (lane <= middle), decay, 0.0)
        near = jnp.sum(later - earlier, axis=1, keepdims=True)
        out_ref[0] = product * widen_column(jnp.exp(near), one)
        scale_ref[0] = jnp.broadcast_to(widen_column(jnp.exp(far), one), (8, width))

    @pl.when(jnp.logical_not(present))
    def _():
        out_ref[...] = jnp.zeros_like(out_ref)
        scale_ref[...] = jnp.zeros_like(scale_ref)


def scan_kernel(me_ref, part_ref, routed_ref, after_ref, out_ref, *, probe_len, heads):
    count, height, width = part_ref.shape
    premise = lax.div(me_ref[0] * height, jnp.int32(DSTATE))
    shape = (DSTATE, width)
    lane = lax.broadcasted_iota(jnp.int32, shape, 0) - premise * heads
    channel = lax.broadcasted_iota(jnp.int32, shape, 1)
    pick = jnp.where(lax.div(channel, jnp.int32(width // heads)) == lane, 1.0, 0.0).astype(BF16)
    state = jnp.zeros((height, width), F32)
    for k in range(count):
        out_ref[k] = state.astype(BF16)
        total = dot(routed_ref[k, probe_len : probe_len + EXTRA, :], pick, 1, 0)
        total = jnp.sum(total[0:8], axis=0, keepdims=True)
        state = state * jnp.exp(total) + part_ref[k].astype(F32)


def apply_kernel(
    table_ref, incoming_ref, routed_ref, local_ref, scale_ref, after_ref, out_ref, done_ref
):
    done_ref[...] = jnp.zeros_like(done_ref)
    slots, probe_len, _ = out_ref.shape
    for slot in range(slots):
        premise = table_ref[4 * slot + 1]
        product = dot(routed_ref[slot, 0:probe_len, :], incoming_ref[premise], 1, 0)
        out_ref[slot] = (product * scale_ref[slot, 0:1, :] + local_ref[slot]).astype(BF16)


def squares(mixed):
    total = mixed[:, 0:128] * mixed[:, 0:128]
    for k in range(1, mixed.shape[1] // 128):
        part = mixed[:, 128 * k : 128 * (k + 1)]
        total = total + part * part
    ones = jnp.ones((8, 128), BF16)
    high, low = pieces(total, 2)
    return dot(ones, high, 1, 1) + dot(ones, low, 1, 1)


def main_kernel(
    in_ref, read_ref, decay_ref, incoming_ref, right_ref, after_ref, out_ref, square_ref
):
    _, length, width = out_ref.shape
    heads = decay_ref.shape[1]
    middle = BLOCK // 2 - 1
    count = length // BLOCK
    one = spread(heads, width)
    twice = spread_twice(one)
    mask = causal(BLOCK, BLOCK)
    line = lax.broadcasted_iota(jnp.int32, (8, BLOCK), 0)
    before = jnp.zeros((heads, 1), F32)
    sums = prefix(decay_ref[0], BLOCK)
    lefts, reaches = [], []
    for k in range(count):
        rows = slice(k * BLOCK, (k + 1) * BLOCK)
        reads = read_ref[0, rows, :]
        gram = jnp.where(mask, dot(reads, in_ref[0, rows, :], 1, 1), 0.0).astype(BF16)
        lefts.append(jnp.concatenate([gram, reads], axis=1))
        mid = sums[k][:, middle : middle + 1]
        reaches.append(widen_column(jnp.exp(before + mid), one))
        before = before + sums[k][:, BLOCK - 1 : BLOCK]
    total = jnp.zeros((8, BLOCK), F32)
    for k in range(count):
        rows = slice(k * BLOCK, (k + 1) * BLOCK)
        product = dot(lefts[k], right_ref[0, k], 1, 0)
        product = product + reaches[k] * dot(read_ref[0, rows, :], incoming_ref[0], 1, 0)
        near = sums[k] - sums[k][:, middle : middle + 1]
        mixed = product * widen(jnp.exp(near), twice)
        out_ref[0, rows, :] = mixed
        total = jnp.where(line == k, squares(mixed), total)
    square_ref[0] = total


def probe_kernel(x_ref, in_ref, read_ref, decay_ref, out_ref, factor_ref, done_ref):
    done_ref[...] = jnp.zeros_like(done_ref)
    probe_dev, length, width = x_ref.shape
    heads = decay_ref.shape[1]
    twice = spread_twice(spread(heads, width))
    mask = causal(length, length)
    for probe in range(probe_dev):
        sums = prefix(decay_ref[probe], length)[0]
        inputs = in_ref[probe]
        scaled = (x_ref[probe].astype(F32) * widen(jnp.exp(-sums), twice)).astype(BF16)
        gram = jnp.where(mask, dot(read_ref[probe], inputs, 1, 1), 0.0).astype(BF16)
        factor = widen(jnp.exp(sums), twice)
        out_ref[probe] = dot(gram, scaled, 1, 0) * factor
        factor_ref[probe] = factor


def join_kernel(
    position_ref,
    me_ref,
    inner_ref,
    factor_ref,
    arrived_ref,
    main_square_ref,
    out_ref,
    square_ref,
    *,
    seq_dev,
):
    probe_dev, length, width = inner_ref.shape
    line = lax.broadcasted_iota(jnp.int32, (8, 128), 0)
    total = jnp.zeros((8, 128), F32)
    pair = 128 // length
    for k in range(probe_dev // pair):
        parts = []
        for probe in range(k * pair, (k + 1) * pair):
            owner = lax.div(position_ref[me_ref[0] * probe_dev + probe], jnp.int32(seq_dev))
            parts.append(inner_ref[probe] + factor_ref[probe] * arrived_ref[owner].astype(F32))
        mixed = jnp.concatenate(parts, axis=0)
        out_ref[128 * k : 128 * (k + 1), :] = mixed
        total = jnp.where(line == k, squares(mixed), total)
    rows = main_square_ref.shape[0]
    for copy in range(square_ref.shape[0]):
        square_ref[copy, 0:rows] = main_square_ref[...]
        square_ref[copy, rows] = total


def norm_kernel(mixed_ref, square_ref, gain_ref, probe_ref, out_ref, probe_out_ref):
    _, length, width = mixed_ref.shape
    row = pl.program_id(0)
    gain = gain_ref[...]

    def rates(index):
        total = square_ref[0, index]
        for copy in range(1, square_ref.shape[0]):
            total = total + square_ref[copy, index]
        return lax.rsqrt(total / DIN + EPSILON)

    rate = rates(row)
    count = length // 128
    if count < 8:
        later = jnp.concatenate([rate[count:], rate[:count]], axis=0)
        rate = jnp.where(pl.program_id(1) == 0, rate, later)
    rate = rate.T
    for k in range(count):
        rows = slice(128 * k, 128 * (k + 1))
        out_ref[0, rows, :] = (mixed_ref[0, rows, :] * rate[:, k : k + 1] * gain).astype(BF16)

    @pl.when((row == 0) & (pl.program_id(1) == 0))
    def _():
        probe_rate = rates(square_ref.shape[1] - 1).T
        for k in range(probe_ref.shape[0] // 128):
            rows = slice(128 * k, 128 * (k + 1))
            probe_out_ref[rows, :] = (
                probe_ref[rows, :] * probe_rate[:, k : k + 1] * gain
            ).astype(BF16)


SMEM = pl.BlockSpec(memory_space=pltpu.SMEM)
VMEM = pl.BlockSpec(memory_space=pltpu.VMEM)


def along(shape, *dims):
    return pl.BlockSpec(
        shape, lambda *at: tuple(at[dims.index(d)] if d in dims else 0 for d in range(len(shape)))
    )


def call(kernel, name, in_specs, out_specs, out_shape, grid=None, scratch=(), limit=58, flops=0, moved=0):
    extra = {} if grid is None else {"grid": grid}
    return pl.pallas_call(
        kernel,
        name=name,
        in_specs=in_specs,
        out_specs=out_specs,
        out_shape=out_shape,
        scratch_shapes=list(scratch),
        compiler_params=pltpu.CompilerParams(vmem_limit_bytes=limit * 1024 * 1024),
        cost_estimate=pl.CostEstimate(flops=flops, bytes_accessed=moved, transcendentals=0),
        **extra,
    )


def shaped(shape, dtype):
    return jax.ShapeDtypeStruct(shape, dtype)


def exchange(value, axis):
    return lax.all_to_all(value, axis, split_axis=0, concat_axis=0, tiled=True)


def local(
    tokens,
    state_inputs,
    state_reads,
    log_decay,
    norm_gain,
    probe_tokens,
    probe_inputs,
    probe_reads,
    probe_decay,
    branch_premise,
    branch_position,
):
    seq = lax.axis_size("seq")
    ring = lax.axis_size("head")
    me = lax.axis_index("seq").astype(jnp.int32).reshape(1)
    row_count, seq_dev, width = tokens.shape
    heads = log_decay.shape[1]
    probe_dev, probe_len, _ = probe_tokens.shape
    height = row_count * DSTATE // seq
    routed_shape = (seq, probe_len + EXTRA, DSTATE)
    count = seq_dev // BLOCK
    depth = BLOCK + DSTATE

    routed, table = call(
        functools.partial(route_kernel, seq_dev=seq_dev),
        "route",
        [SMEM, SMEM, SMEM, along(probe_reads.shape), along(log_decay.shape)],
        [along(routed_shape), SMEM],
        [shaped(routed_shape, BF16), shaped((4 * seq,), jnp.int32)],
        (1,),
        moved=800_000,
    )(branch_position, branch_premise, me, probe_reads, log_decay)
    routed = exchange(routed, "seq")

    x_spec = along((1, seq_dev, width), 0)
    in_spec = along((1, seq_dev, DSTATE), 0)
    decay_spec = along((1, heads, seq_dev), 0)
    ends = call(
        end_kernel,
        "ends",
        [x_spec, in_spec, decay_spec],
        along((1, DSTATE, width), 0),
        shaped((row_count, DSTATE, width), BF16),
        (row_count,),
        [pltpu.VMEM((seq_dev, width), BF16)],
        flops=4_000_000_000,
        moved=20_000_000,
    )(tokens, state_inputs, log_decay)
    parts = exchange(ends.reshape(seq, height, width), "seq")

    token = shaped((8, 128), F32)
    token_spec = pl.BlockSpec((8, 128), lambda *at: (0, 0))
    right, built = call(
        build_kernel,
        "build",
        [x_spec, in_spec, decay_spec],
        [along((1, count, depth, width), 0), token_spec],
        [shaped((row_count, count, depth, width), BF16), token],
        (row_count,),
        flops=5_000_000_000,
        moved=40_000_000,
    )(tokens, state_inputs, log_decay)

    starts = call(
        functools.partial(scan_kernel, probe_len=probe_len, heads=heads),
        "scan",
        [SMEM, VMEM, VMEM, VMEM],
        VMEM,
        shaped((seq, height, width), BF16),
        limit=16,
        flops=1_000_000_000,
        moved=2_500_000,
    )(me, parts, routed, built)
    incoming = exchange(starts, "seq").reshape(row_count, DSTATE, width)

    local_part, scale = pl.pallas_call(
        branch_kernel,
        name="branch",
        grid_spec=pltpu.PrefetchScalarGridSpec(
            num_scalar_prefetch=1,
            grid=(seq,),
            in_specs=[
                pl.BlockSpec(
                    (1, 1, depth, width), lambda i, t: (t[4 * i + 1], t[4 * i + 2], 0, 0)
                ),
                pl.BlockSpec((1, BLOCK, DSTATE), lambda i, t: (t[4 * i + 1], t[4 * i + 2], 0)),
                pl.BlockSpec((1, heads, seq_dev), lambda i, t: (t[4 * i + 1], 0, 0)),
                pl.BlockSpec((1,) + routed_shape[1:], lambda i, t: (i, 0, 0)),
            ],
            out_specs=[
                pl.BlockSpec((1, probe_len, width), lambda i, t: (i, 0, 0)),
                pl.BlockSpec((1, 8, width), lambda i, t: (i, 0, 0)),
            ],
        ),
        out_shape=[shaped((seq, probe_len, width), F32), shaped((seq, 8, width), F32)],
        compiler_params=pltpu.CompilerParams(vmem_limit_bytes=48 * 1024 * 1024),
        cost_estimate=pl.CostEstimate(
            flops=1_000_000_000, bytes_accessed=20_000_000, transcendentals=0
        ),
    )(table, right, state_inputs, log_decay, routed)
    inner, factor, probed = call(
        probe_kernel,
        "probes",
        [VMEM] * 4,
        [VMEM] * 3,
        [shaped(probe_tokens.shape, F32)] * 2 + [token],
        limit=40,
        flops=1_000_000_000,
        moved=8_000_000,
    )(probe_tokens, probe_inputs, probe_reads, probe_decay)

    answers, applied = call(
        apply_kernel,
        "apply",
        [SMEM, VMEM, VMEM, VMEM, VMEM, VMEM],
        [VMEM, VMEM],
        [shaped((seq, probe_len, width), BF16), token],
        limit=40,
        flops=1_000_000_000,
        moved=8_000_000,
    )(table, incoming, routed, local_part, scale, probed)
    arrived = exchange(answers, "seq")

    mixed, square = call(
        main_kernel,
        "main",
        [
            in_spec,
            in_spec,
            decay_spec,
            along((1, DSTATE, width), 0),
            along((1, count, depth, width), 0),
            token_spec,
        ],
        [x_spec, along((1, 8, 128), 0)],
        [shaped(tokens.shape, F32), shaped((row_count, 8, 128), F32)],
        (row_count,),
        limit=40,
        flops=12_000_000_000,
        moved=60_000_000,
    )(state_inputs, state_reads, log_decay, incoming, right, applied)

    probe_rows = (probe_dev * probe_len, width)
    square_shape = (ring, row_count + 1, 8, 128)
    probe_mixed, square = call(
        functools.partial(join_kernel, seq_dev=seq_dev),
        "join",
        [SMEM, SMEM, VMEM, VMEM, VMEM, VMEM],
        [VMEM, VMEM],
        [shaped(probe_rows, F32), shaped(square_shape, F32)],
        limit=40,
        flops=1_000_000,
        moved=5_000_000,
    )(branch_position, me, inner, factor, arrived, square)
    square = exchange(square, "head")

    half_spec = along((1, seq_dev // 2, width), 0, 1)
    premise_out, probe_out = call(
        norm_kernel,
        "norm",
        [
            half_spec,
            along(square_shape),
            along((1, width)),
            along(probe_rows),
        ],
        [half_spec, along(probe_rows)],
        [shaped(tokens.shape, BF16), shaped(probe_rows, BF16)],
        (row_count, 2),
        limit=48,
        flops=1_000_000_000,
        moved=30_000_000,
    )(mixed, square, norm_gain.reshape(1, width), probe_mixed)
    return (premise_out, probe_out.reshape(probe_dev, probe_len, width))


def solution(mesh):
    return jax.shard_map(
        local,
        mesh=mesh,
        in_specs=(
            P(None, "seq", "head"),
            P(None, "seq", "head"),
            P(None, "seq", "head"),
            P(None, "head", "seq"),
            P("head"),
            P("seq", None, "head"),
            P("seq", None, "head"),
            P("seq", None, "head"),
            P("seq", "head", None),
            P(),
            P(),
        ),
        out_specs=(P(None, "seq", "head"), P("seq", None, "head")),
        check_vma=False,
    )
```

```python
import functools

import jax
import jax.numpy as jnp
from jax import lax
from jax.experimental import pallas as pl
from jax.experimental.pallas import tpu as pltpu
from jax.sharding import PartitionSpec as P

F32 = jnp.float32
BF16 = jnp.bfloat16
DSTATE = 128
DIN = 8192
EPSILON = 1e-05
BLOCK = 128
EXTRA = 16


def dot(left, right, left_dim, right_dim, precision=None):
    return lax.dot_general(
        left,
        right,
        (((left_dim,), (right_dim,)), ((), ())),
        precision=precision,
        preferred_element_type=F32,
    )


def pieces(value, count):
    parts = []
    for _ in range(count):
        part = value.astype(BF16)
        parts.append(part)
        value = value - part.astype(F32)
    return parts


def spread(heads, width):
    shape = (heads, width)
    head = lax.broadcasted_iota(jnp.int32, shape, 0)
    channel = lax.broadcasted_iota(jnp.int32, shape, 1)
    per_head = width // heads
    return jnp.where(lax.div(channel, jnp.int32(per_head)) == head, 1.0, 0.0).astype(F32)


def spread_twice(one):
    half = one.astype(BF16)
    return jnp.concatenate([half, half], axis=0)


def widen(value, twice):
    return dot(jnp.concatenate(pieces(value, 2), axis=0), twice, 0, 0)


def widen_column(column, one):
    return jnp.sum(column * one, axis=0, keepdims=True)


def prefix(decay, length):
    heads = decay.shape[0]
    count = decay.shape[1] // length
    parts = pieces(decay, 3)
    rows = [part[:, k * length : (k + 1) * length] for k in range(count) for part in parts]
    shape = (length, length)
    upto = (
        lax.broadcasted_iota(jnp.int32, shape, 0) <= lax.broadcasted_iota(jnp.int32, shape, 1)
    )
    total = dot(jnp.concatenate(rows, axis=0), jnp.where(upto, 1.0, 0.0).astype(BF16), 1, 0)
    out = []
    for k in range(count):
        base = 3 * heads * k
        out.append(
            total[base : base + heads]
            + total[base + heads : base + 2 * heads]
            + total[base + 2 * heads : base + 3 * heads]
        )
    return out


def causal(queries, keys):
    shape = (queries, keys)
    return lax.broadcasted_iota(jnp.int32, shape, 0) >= lax.broadcasted_iota(jnp.int32, shape, 1)


def route_kernel(
    position_ref, premise_ref, me_ref, reads_ref, decay_ref, out_ref, table_ref, *, seq_dev
):
    slots = out_ref.shape[0]
    probe_dev, probe_len, _ = reads_ref.shape
    rows, heads, length = decay_ref.shape
    decay = decay_ref[...].reshape(rows * heads, length)
    ones = jnp.ones((EXTRA, length), BF16)
    fill = jnp.zeros((DSTATE - rows * heads, length), BF16)
    total = 0.0
    for part in pieces(decay, 3):
        total = total + dot(ones, jnp.concatenate([part, fill], axis=0), 1, 1)
    row = lax.broadcasted_iota(jnp.int32, (EXTRA, DSTATE), 0)
    block = jnp.zeros((EXTRA, DSTATE), F32)
    for index, part in enumerate(pieces(total, 3)):
        block = jnp.where(row == index, part.astype(F32), block)
    block = block.astype(BF16)
    nothing = jnp.zeros((probe_len, DSTATE), BF16)
    for slot in range(slots):
        out_ref[slot, 0:probe_len, :] = nothing
        out_ref[slot, probe_len : probe_len + EXTRA, :] = block
    for probe in range(probe_dev):
        owner = lax.div(position_ref[me_ref[0] * probe_dev + probe], jnp.int32(seq_dev))
        out_ref[owner, 0:probe_len, :] = reads_ref[probe]
    me = me_ref[0]
    for slot in range(slots):
        offset = jnp.int32(0)
        premise = jnp.int32(0)
        present = jnp.int32(0)
        for probe in range(probe_dev):
            position = position_ref[slot * probe_dev + probe]
            here = lax.div(position, jnp.int32(seq_dev)) == me
            offset = jnp.where(here, position - me * seq_dev, offset)
            premise = jnp.where(here, premise_ref[slot * probe_dev + probe], premise)
            present = jnp.where(here, jnp.int32(1), present)
        block = lax.div(offset, jnp.int32(BLOCK))
        table_ref[4 * slot] = present
        table_ref[4 * slot + 1] = premise
        table_ref[4 * slot + 2] = block
        table_ref[4 * slot + 3] = offset - block * BLOCK


def end_kernel(x_ref, in_ref, decay_ref, out_ref, scaled_ref):
    _, length, width = x_ref.shape
    heads = decay_ref.shape[1]
    twice = spread_twice(spread(heads, width))
    sums = prefix(decay_ref[0], BLOCK)
    after = jnp.zeros((heads, 1), F32)
    for k in reversed(range(length // BLOCK)):
        rows = slice(k * BLOCK, (k + 1) * BLOCK)
        last = sums[k][:, BLOCK - 1 : BLOCK]
        factor = widen(jnp.exp((last - sums[k]) + after), twice)
        scaled_ref[rows, :] = (x_ref[0, rows, :].astype(F32) * factor).astype(BF16)
        after = after + last
    out_ref[0] = dot(in_ref[0], scaled_ref[...], 0, 0).astype(BF16)


def chain_factors(sums, one):
    middle = BLOCK // 2 - 1
    factors = []
    tail = None
    for k in range(len(sums)):
        mid = sums[k][:, middle : middle + 1]
        step = mid if tail is None else tail + mid
        factors.append(widen_column(jnp.exp(step), one))
        tail = sums[k][:, BLOCK - 1 : BLOCK] - mid
    return factors


def build_kernel(x_ref, in_ref, decay_ref, out_ref, done_ref):
    _, length, width = x_ref.shape
    heads = decay_ref.shape[1]
    middle = BLOCK // 2 - 1
    one = spread(heads, width)
    twice = spread_twice(one)
    sums = prefix(decay_ref[0], BLOCK)
    factors = chain_factors(sums, one)
    count = length // BLOCK
    done_ref[...] = jnp.zeros_like(done_ref)
    for k in range(count):
        rows = slice(k * BLOCK, (k + 1) * BLOCK)
        near = sums[k] - sums[k][:, middle : middle + 1]
        factor = widen(jnp.exp(-near), twice)
        out_ref[0, k, 0:BLOCK, :] = (x_ref[0, rows, :].astype(F32) * factor).astype(BF16)
    out_ref[0, 0, BLOCK : BLOCK + DSTATE, :] = jnp.zeros((DSTATE, width), BF16)
    written = [
        dot(in_ref[0, k * BLOCK : (k + 1) * BLOCK, :], out_ref[0, k, 0:BLOCK, :], 0, 0)
        for k in range(count - 1)
    ]
    state = written[0]
    for k in range(1, count):
        state = state * factors[k]
        out_ref[0, k, BLOCK : BLOCK + DSTATE, :] = state.astype(BF16)
        if k < count - 1:
            state = state + written[k]


def branch_kernel(table_ref, *refs, step):
    rights, inputs, decays = (refs[i * step : (i + 1) * step] for i in range(3))
    routed_ref, out_ref, scale_ref = refs[3 * step :]
    _, probe_len, width = out_ref.shape
    _, heads, length = decays[0].shape
    one = spread(heads, width)
    lane = lax.broadcasted_iota(jnp.int32, (heads, length), 1)
    key = lax.broadcasted_iota(jnp.int32, (probe_len, BLOCK), 1)
    lefts = []
    for index in range(step):
        slot = pl.program_id(0) * step + index
        reads = routed_ref[index, 0:probe_len, :]
        keep = key <= table_ref[4 * slot + 3]
        gram = jnp.where(keep, dot(reads, inputs[index][0], 1, 1), 0.0).astype(BF16)
        lefts.append(jnp.concatenate([gram, reads], axis=1))
    for index in range(step):
        slot = pl.program_id(0) * step + index
        start = table_ref[4 * slot + 2] * BLOCK
        offset = start + table_ref[4 * slot + 3]
        middle = start + BLOCK // 2 - 1
        decay = decays[index][0]
        far = jnp.sum(jnp.where(lane <= offset, decay, 0.0), axis=1, keepdims=True)
        later = jnp.where((lane > middle) & (lane <= offset), decay, 0.0)
        earlier = jnp.where((lane > offset) & (lane <= middle), decay, 0.0)
        near = jnp.sum(later - earlier, axis=1, keepdims=True)
        product = dot(lefts[index], rights[index][0, 0], 1, 0)
        out_ref[index] = product * widen_column(jnp.exp(near), one)
        scale_ref[index] = jnp.broadcast_to(widen_column(jnp.exp(far), one), (8, width))


def scan_kernel(me_ref, part_ref, routed_ref, built_ref, probed_ref, out_ref, *, probe_len, heads):
    count, height, width = part_ref.shape
    premise = lax.div(me_ref[0] * height, jnp.int32(DSTATE))
    shape = (DSTATE, width)
    lane = lax.broadcasted_iota(jnp.int32, shape, 0) - premise * heads
    channel = lax.broadcasted_iota(jnp.int32, shape, 1)
    pick = jnp.where(lax.div(channel, jnp.int32(width // heads)) == lane, 1.0, 0.0).astype(BF16)
    state = jnp.zeros((height, width), F32)
    for k in range(count):
        out_ref[k] = state.astype(BF16)
        total = dot(routed_ref[k, probe_len : probe_len + EXTRA, :], pick, 1, 0)
        total = jnp.sum(total[0:8], axis=0, keepdims=True)
        state = state * jnp.exp(total) + part_ref[k].astype(F32)


def apply_kernel(table_ref, incoming_ref, routed_ref, local_ref, scale_ref, out_ref, done_ref):
    step, probe_len, _ = out_ref.shape
    done_ref[...] = jnp.zeros_like(done_ref)
    for index in range(step):
        premise = table_ref[4 * (pl.program_id(0) * step + index) + 1]
        product = dot(routed_ref[index, 0:probe_len, :], incoming_ref[premise], 1, 0)
        out_ref[index] = (product * scale_ref[index, 0:1, :] + local_ref[index]).astype(BF16)


def squares(mixed):
    total = mixed[:, 0:128] * mixed[:, 0:128]
    for k in range(1, mixed.shape[1] // 128):
        part = mixed[:, 128 * k : 128 * (k + 1)]
        total = total + part * part
    ones = jnp.ones((8, 128), BF16)
    high, low = pieces(total, 2)
    return dot(ones, high, 1, 1) + dot(ones, low, 1, 1)


def main_kernel(
    in_ref, read_ref, decay_ref, incoming_ref, right_ref, gain_ref, after_ref, out_ref, square_ref
):
    _, length, width = out_ref.shape
    heads = decay_ref.shape[1]
    middle = BLOCK // 2 - 1
    count = length // BLOCK
    one = spread(heads, width)
    twice = spread_twice(one)
    mask = causal(BLOCK, BLOCK)
    line = lax.broadcasted_iota(jnp.int32, (8, BLOCK), 0)
    before = jnp.zeros((heads, 1), F32)
    sums = prefix(decay_ref[0], BLOCK)
    lefts, reaches = [], []
    for k in range(count):
        rows = slice(k * BLOCK, (k + 1) * BLOCK)
        reads = read_ref[0, rows, :]
        gram = jnp.where(mask, dot(reads, in_ref[0, rows, :], 1, 1), 0.0).astype(BF16)
        lefts.append(jnp.concatenate([gram, reads], axis=1))
        mid = sums[k][:, middle : middle + 1]
        reaches.append(widen_column(jnp.exp(before + mid), one))
        before = before + sums[k][:, BLOCK - 1 : BLOCK]
    total = jnp.zeros((8, BLOCK), F32)
    for k in range(count):
        rows = slice(k * BLOCK, (k + 1) * BLOCK)
        product = dot(lefts[k], right_ref[0, k], 1, 0)
        product = product + reaches[k] * dot(read_ref[0, rows, :], incoming_ref[0], 1, 0)
        near = sums[k] - sums[k][:, middle : middle + 1]
        mixed = product * widen(jnp.exp(near), twice)
        out_ref[0, rows, :] = mixed * gain_ref[...]
        total = jnp.where(line == k, squares(mixed), total)
    square_ref[0] = total


def probe_kernel(x_ref, in_ref, read_ref, decay_ref, out_ref, factor_ref, done_ref):
    done_ref[...] = jnp.zeros_like(done_ref)
    probe_dev, length, width = x_ref.shape
    heads = decay_ref.shape[1]
    twice = spread_twice(spread(heads, width))
    mask = causal(length, length)
    for probe in range(probe_dev):
        sums = prefix(decay_ref[probe], length)[0]
        inputs = in_ref[probe]
        scaled = (x_ref[probe].astype(F32) * widen(jnp.exp(-sums), twice)).astype(BF16)
        gram = jnp.where(mask, dot(read_ref[probe], inputs, 1, 1), 0.0).astype(BF16)
        factor = widen(jnp.exp(sums), twice)
        out_ref[probe] = dot(gram, scaled, 1, 0) * factor
        factor_ref[probe] = factor


def join_kernel(
    position_ref, me_ref, inner_ref, factor_ref, gain_ref, arrived_ref, out_ref, square_ref, *, seq_dev
):
    pair, length, width = inner_ref.shape
    row = pl.program_id(0)
    probe_dev = pair * pl.num_programs(0)
    parts = []
    for index in range(pair):
        probe = row * pair + index
        owner = lax.div(position_ref[me_ref[0] * probe_dev + probe], jnp.int32(seq_dev))
        parts.append(inner_ref[index] + factor_ref[index] * arrived_ref[owner].astype(F32))
    mixed = jnp.concatenate(parts, axis=0)
    out_ref[...] = mixed * gain_ref[...]
    total = squares(mixed)
    line = lax.broadcasted_iota(jnp.int32, (8, 128), 0)

    @pl.when(row == 0)
    def _():
        square_ref[...] = jnp.zeros_like(square_ref)

    for copy in range(square_ref.shape[0]):
        square_ref[copy] = jnp.where(line == row, total, square_ref[copy])


def norm_kernel(mixed_ref, *refs):
    out_ref = refs[-1]
    total = 0.0
    for ref in refs[:-1]:
        total = total + jnp.sum(ref[...].reshape(-1, 8, 128), axis=0)
    rate = lax.rsqrt(total / DIN + EPSILON).T
    for k in range(mixed_ref.shape[1] // 128):
        rows = slice(128 * k, 128 * (k + 1))
        out_ref[0, rows, :] = (mixed_ref[0, rows, :] * rate[:, k : k + 1]).astype(BF16)


SMEM = pl.BlockSpec(memory_space=pltpu.SMEM)
VMEM = pl.BlockSpec(memory_space=pltpu.VMEM)
ANY = pl.BlockSpec(memory_space=pl.ANY)


def along(shape, *dims):
    return pl.BlockSpec(
        shape, lambda *at: tuple(at[dims.index(d)] if d in dims else 0 for d in range(len(shape)))
    )


def call(kernel, name, in_specs, out_specs, out_shape, grid=None, scratch=(), limit=58, flops=0, moved=0):
    extra = {} if grid is None else {"grid": grid}
    return pl.pallas_call(
        kernel,
        name=name,
        in_specs=in_specs,
        out_specs=out_specs,
        out_shape=out_shape,
        scratch_shapes=list(scratch),
        compiler_params=pltpu.CompilerParams(vmem_limit_bytes=limit * 1024 * 1024),
        cost_estimate=pl.CostEstimate(flops=flops, bytes_accessed=moved, transcendentals=0),
        **extra,
    )


def shaped(shape, dtype):
    return jax.ShapeDtypeStruct(shape, dtype)


def exchange(value, axis):
    return lax.all_to_all(value, axis, split_axis=0, concat_axis=0, tiled=True)


def local(
    tokens,
    state_inputs,
    state_reads,
    log_decay,
    norm_gain,
    probe_tokens,
    probe_inputs,
    probe_reads,
    probe_decay,
    branch_premise,
    branch_position,
):
    seq = lax.axis_size("seq")
    ring = lax.axis_size("head")
    me = lax.axis_index("seq").astype(jnp.int32).reshape(1)
    row_count, seq_dev, width = tokens.shape
    heads = log_decay.shape[1]
    probe_dev, probe_len, _ = probe_tokens.shape
    height = row_count * DSTATE // seq
    routed_shape = (seq, probe_len + EXTRA, DSTATE)
    count = seq_dev // BLOCK
    depth = BLOCK + DSTATE

    routed, table = call(
        functools.partial(route_kernel, seq_dev=seq_dev),
        "route",
        [SMEM, SMEM, SMEM, along(probe_reads.shape), along(log_decay.shape)],
        [along(routed_shape), SMEM],
        [shaped(routed_shape, BF16), shaped((4 * seq,), jnp.int32)],
        (1,),
        moved=800_000,
    )(branch_position, branch_premise, me, probe_reads, log_decay)
    routed = exchange(routed, "seq")

    x_spec = along((1, seq_dev, width), 0)
    in_spec = along((1, seq_dev, DSTATE), 0)
    decay_spec = along((1, heads, seq_dev), 0)
    ends = call(
        end_kernel,
        "ends",
        [x_spec, in_spec, decay_spec],
        along((1, DSTATE, width), 0),
        shaped((row_count, DSTATE, width), BF16),
        (row_count,),
        [pltpu.VMEM((seq_dev, width), BF16)],
        flops=4_000_000_000,
        moved=20_000_000,
    )(tokens, state_inputs, log_decay)
    parts = exchange(ends.reshape(seq, height, width), "seq")

    token = shaped((8, 128), F32)
    token_spec = pl.BlockSpec((8, 128), lambda *at: (0, 0))
    right, built = call(
        build_kernel,
        "build",
        [x_spec, in_spec, decay_spec],
        [along((1, count, depth, width), 0), token_spec],
        [shaped((row_count, count, depth, width), BF16), token],
        (row_count,),
        flops=5_000_000_000,
        moved=40_000_000,
    )(tokens, state_inputs, log_decay)

    probe_rows = probe_dev * probe_len
    inner, factor, probed = call(
        probe_kernel,
        "probes",
        [along(part.shape) for part in (probe_tokens, probe_inputs, probe_reads, probe_decay)],
        [along(probe_tokens.shape)] * 2 + [token_spec],
        [shaped(probe_tokens.shape, F32)] * 2 + [token],
        (1,),
        flops=1_000_000_000,
        moved=8_000_000,
    )(probe_tokens, probe_inputs, probe_reads, probe_decay)

    starts = call(
        functools.partial(scan_kernel, probe_len=probe_len, heads=heads),
        "scan",
        [SMEM, VMEM, along(routed_shape), ANY, ANY],
        along((seq, height, width)),
        shaped((seq, height, width), BF16),
        (1,),
        limit=48,
        flops=1_000_000_000,
        moved=2_500_000,
    )(me, parts, routed, built, probed)
    incoming = exchange(starts, "seq").reshape(row_count, DSTATE, width)

    step = 4

    def picked(shape, index, blocked):
        def at(i, t):
            base = 4 * (step * i + index)
            first = (t[base + 1], t[base + 2]) if blocked else (t[base + 1],)
            return first + (0,) * (len(shape) - len(first))

        return pl.BlockSpec(shape, at)

    local_part, scale = pl.pallas_call(
        functools.partial(branch_kernel, step=step),
        name="branch",
        grid_spec=pltpu.PrefetchScalarGridSpec(
            num_scalar_prefetch=1,
            grid=(seq // step,),
            in_specs=[picked((1, 1, depth, width), i, True) for i in range(step)]
            + [picked((1, BLOCK, DSTATE), i, True) for i in range(step)]
            + [picked((1, heads, seq_dev), i, False) for i in range(step)]
            + [along((step,) + routed_shape[1:], 0)],
            out_specs=[along((step, probe_len, width), 0), along((step, 8, width), 0)],
        ),
        out_shape=[shaped((seq, probe_len, width), F32), shaped((seq, 8, width), F32)],
        compiler_params=pltpu.CompilerParams(vmem_limit_bytes=58 * 1024 * 1024),
        cost_estimate=pl.CostEstimate(
            flops=1_000_000_000, bytes_accessed=20_000_000, transcendentals=0
        ),
    )(
        table,
        *[right] * step,
        *[state_inputs] * step,
        *[log_decay] * step,
        routed,
    )

    answers, applied = call(
        apply_kernel,
        "apply",
        [SMEM, VMEM]
        + [
            along(shape, 0)
            for shape in (
                (step,) + routed_shape[1:],
                (step, probe_len, width),
                (step, 8, width),
            )
        ],
        [along((step, probe_len, width), 0), token_spec],
        [shaped((seq, probe_len, width), BF16), token],
        (seq // step,),
        limit=48,
        flops=1_000_000_000,
        moved=8_000_000,
    )(table, incoming, routed, local_part, scale)
    arrived = exchange(answers, "seq")

    gain = norm_gain.reshape(1, width)
    square_spec = along((1, 8, 128), 0)
    square_shape = (row_count, 8, 128)
    mixed, square = call(
        main_kernel,
        "main",
        [
            in_spec,
            in_spec,
            decay_spec,
            along((1, DSTATE, width), 0),
            along((1, count, depth, width), 0),
            along((1, width)),
            ANY,
        ],
        [x_spec, square_spec],
        [shaped(tokens.shape, F32), shaped(square_shape, F32)],
        (row_count,),
        flops=12_000_000_000,
        moved=60_000_000,
    )(state_inputs, state_reads, log_decay, incoming, right, gain, applied)
    shared = [square] + [
        lax.ppermute(square, "head", [(i, (i + turn) % ring) for i in range(ring)])
        for turn in range(1, ring)
    ]

    probe_mixed, probe_square = call(
        functools.partial(join_kernel, seq_dev=seq_dev),
        "join",
        [
            SMEM,
            SMEM,
            along((128 // probe_len, probe_len, width), 0),
            along((128 // probe_len, probe_len, width), 0),
            along((1, width)),
            VMEM,
        ],
        [along((128, width), 0), along((ring, 8, 128))],
        [shaped((probe_rows, width), F32), shaped((ring, 8, 128), F32)],
        (probe_rows // 128,),
        limit=48,
        flops=1_000_000,
        moved=5_000_000,
    )(branch_position, me, inner, factor, gain, arrived)
    probe_square = exchange(probe_square, "head")

    premise_out = call(
        norm_kernel,
        "norm",
        [x_spec] + [square_spec] * ring,
        x_spec,
        shaped(tokens.shape, BF16),
        (row_count,),
        limit=50,
        flops=1_000_000_000,
        moved=30_000_000,
    )(mixed, *shared)
    probe_shape = (1, probe_rows, width)
    probe_out = call(
        norm_kernel,
        "probe_norm",
        [along(probe_shape), along((ring, 8, 128))],
        along(probe_shape),
        shaped(probe_shape, BF16),
        (1,),
        limit=54,
        flops=1_000_000,
        moved=2_000_000,
    )(probe_mixed.reshape(probe_shape), probe_square)
    return (premise_out, probe_out.reshape(probe_dev, probe_len, width))


def solution(mesh):
    return jax.shard_map(
        local,
        mesh=mesh,
        in_specs=(
            P(None, "seq", "head"),
            P(None, "seq", "head"),
            P(None, "seq", "head"),
            P(None, "head", "seq"),
            P("head"),
            P("seq", None, "head"),
            P("seq", None, "head"),
            P("seq", None, "head"),
            P("seq", "head", None),
            P(),
            P(),
        ),
        out_specs=(P(None, "seq", "head"), P("seq", None, "head")),
        check_vma=False,
    )
```

```python
import functools

import jax
import jax.numpy as jnp
from jax import lax
from jax.experimental import pallas as pl
from jax.experimental.pallas import tpu as pltpu
from jax.sharding import PartitionSpec as P

F32 = jnp.float32
BF16 = jnp.bfloat16
DSTATE = 128
DIN = 8192
EPSILON = 1e-05
BLOCK = 128
EXTRA = 16


def dot(left, right, left_dim, right_dim, precision=None):
    return lax.dot_general(
        left,
        right,
        (((left_dim,), (right_dim,)), ((), ())),
        precision=precision,
        preferred_element_type=F32,
    )


def pieces(value, count):
    parts = []
    for _ in range(count):
        part = value.astype(BF16)
        parts.append(part)
        value = value - part.astype(F32)
    return parts


def spread(heads, width):
    shape = (heads, width)
    head = lax.broadcasted_iota(jnp.int32, shape, 0)
    channel = lax.broadcasted_iota(jnp.int32, shape, 1)
    per_head = width // heads
    return jnp.where(lax.div(channel, jnp.int32(per_head)) == head, 1.0, 0.0).astype(F32)


def spread_twice(one):
    half = one.astype(BF16)
    return jnp.concatenate([half, half], axis=0)


def widen(value, twice):
    return dot(jnp.concatenate(pieces(value, 2), axis=0), twice, 0, 0)


def widen_column(column, one):
    return jnp.sum(column * one, axis=0, keepdims=True)


def prefix(decay, length):
    heads = decay.shape[0]
    count = decay.shape[1] // length
    parts = pieces(decay, 3)
    rows = [part[:, k * length : (k + 1) * length] for k in range(count) for part in parts]
    shape = (length, length)
    upto = (
        lax.broadcasted_iota(jnp.int32, shape, 0) <= lax.broadcasted_iota(jnp.int32, shape, 1)
    )
    total = dot(jnp.concatenate(rows, axis=0), jnp.where(upto, 1.0, 0.0).astype(BF16), 1, 0)
    out = []
    for k in range(count):
        base = 3 * heads * k
        out.append(
            total[base : base + heads]
            + total[base + heads : base + 2 * heads]
            + total[base + 2 * heads : base + 3 * heads]
        )
    return out


def causal(queries, keys):
    shape = (queries, keys)
    return lax.broadcasted_iota(jnp.int32, shape, 0) >= lax.broadcasted_iota(jnp.int32, shape, 1)


def route_kernel(
    position_ref, premise_ref, me_ref, reads_ref, decay_ref, out_ref, table_ref, *, seq_dev
):
    slots = out_ref.shape[0]
    probe_dev, probe_len, _ = reads_ref.shape
    rows, heads, length = decay_ref.shape
    decay = decay_ref[...].reshape(rows * heads, length)
    ones = jnp.ones((EXTRA, length), BF16)
    fill = jnp.zeros((DSTATE - rows * heads, length), BF16)
    total = 0.0
    for part in pieces(decay, 3):
        total = total + dot(ones, jnp.concatenate([part, fill], axis=0), 1, 1)
    row = lax.broadcasted_iota(jnp.int32, (EXTRA, DSTATE), 0)
    block = jnp.zeros((EXTRA, DSTATE), F32)
    for index, part in enumerate(pieces(total, 3)):
        block = jnp.where(row == index, part.astype(F32), block)
    block = block.astype(BF16)
    nothing = jnp.zeros((probe_len, DSTATE), BF16)
    for slot in range(slots):
        out_ref[slot, 0:probe_len, :] = nothing
        out_ref[slot, probe_len : probe_len + EXTRA, :] = block
    for probe in range(probe_dev):
        owner = lax.div(position_ref[me_ref[0] * probe_dev + probe], jnp.int32(seq_dev))
        out_ref[owner, 0:probe_len, :] = reads_ref[probe]
    me = me_ref[0]
    for slot in range(slots):
        offset = jnp.int32(0)
        premise = jnp.int32(0)
        present = jnp.int32(0)
        for probe in range(probe_dev):
            position = position_ref[slot * probe_dev + probe]
            here = lax.div(position, jnp.int32(seq_dev)) == me
            offset = jnp.where(here, position - me * seq_dev, offset)
            premise = jnp.where(here, premise_ref[slot * probe_dev + probe], premise)
            present = jnp.where(here, jnp.int32(1), present)
        block = lax.div(offset, jnp.int32(BLOCK))
        table_ref[4 * slot] = present
        table_ref[4 * slot + 1] = premise
        table_ref[4 * slot + 2] = block
        table_ref[4 * slot + 3] = offset - block * BLOCK


def end_kernel(x_ref, in_ref, decay_ref, out_ref, scaled_ref):
    _, length, width = x_ref.shape
    heads = decay_ref.shape[1]
    twice = spread_twice(spread(heads, width))
    sums = prefix(decay_ref[0], BLOCK)
    after = jnp.zeros((heads, 1), F32)
    for k in reversed(range(length // BLOCK)):
        rows = slice(k * BLOCK, (k + 1) * BLOCK)
        last = sums[k][:, BLOCK - 1 : BLOCK]
        factor = widen(jnp.exp((last - sums[k]) + after), twice)
        scaled_ref[rows, :] = (x_ref[0, rows, :].astype(F32) * factor).astype(BF16)
        after = after + last
    out_ref[0] = dot(in_ref[0], scaled_ref[...], 0, 0).astype(BF16)


def chain_factors(sums, one):
    middle = BLOCK // 2 - 1
    factors = []
    tail = None
    for k in range(len(sums)):
        mid = sums[k][:, middle : middle + 1]
        step = mid if tail is None else tail + mid
        factors.append(widen_column(jnp.exp(step), one))
        tail = sums[k][:, BLOCK - 1 : BLOCK] - mid
    return factors


def build_kernel(x_ref, in_ref, decay_ref, out_ref, done_ref):
    _, length, width = x_ref.shape
    heads = decay_ref.shape[1]
    middle = BLOCK // 2 - 1
    one = spread(heads, width)
    twice = spread_twice(one)
    sums = prefix(decay_ref[0], BLOCK)
    factors = chain_factors(sums, one)
    count = length // BLOCK
    done_ref[...] = jnp.zeros_like(done_ref)
    for k in range(count):
        rows = slice(k * BLOCK, (k + 1) * BLOCK)
        near = sums[k] - sums[k][:, middle : middle + 1]
        factor = widen(jnp.exp(-near), twice)
        out_ref[0, k, 0:BLOCK, :] = (x_ref[0, rows, :].astype(F32) * factor).astype(BF16)
    out_ref[0, 0, BLOCK : BLOCK + DSTATE, :] = jnp.zeros((DSTATE, width), BF16)
    written = [
        dot(in_ref[0, k * BLOCK : (k + 1) * BLOCK, :], out_ref[0, k, 0:BLOCK, :], 0, 0)
        for k in range(count - 1)
    ]
    state = written[0]
    for k in range(1, count):
        state = state * factors[k]
        out_ref[0, k, BLOCK : BLOCK + DSTATE, :] = state.astype(BF16)
        if k < count - 1:
            state = state + written[k]


def branch_kernel(table_ref, *refs, step):
    rights, inputs, decays = (refs[i * step : (i + 1) * step] for i in range(3))
    routed_ref, out_ref, scale_ref = refs[3 * step :]
    _, probe_len, width = out_ref.shape
    _, heads, length = decays[0].shape
    one = spread(heads, width)
    lane = lax.broadcasted_iota(jnp.int32, (heads, length), 1)
    key = lax.broadcasted_iota(jnp.int32, (probe_len, BLOCK), 1)
    lefts = []
    for index in range(step):
        slot = pl.program_id(0) * step + index
        reads = routed_ref[index, 0:probe_len, :]
        keep = key <= table_ref[4 * slot + 3]
        gram = jnp.where(keep, dot(reads, inputs[index][0], 1, 1), 0.0).astype(BF16)
        lefts.append(jnp.concatenate([gram, reads], axis=1))
    for index in range(step):
        slot = pl.program_id(0) * step + index
        start = table_ref[4 * slot + 2] * BLOCK
        offset = start + table_ref[4 * slot + 3]
        middle = start + BLOCK // 2 - 1
        decay = decays[index][0]
        far = jnp.sum(jnp.where(lane <= offset, decay, 0.0), axis=1, keepdims=True)
        later = jnp.where((lane > middle) & (lane <= offset), decay, 0.0)
        earlier = jnp.where((lane > offset) & (lane <= middle), decay, 0.0)
        near = jnp.sum(later - earlier, axis=1, keepdims=True)
        product = dot(lefts[index], rights[index][0, 0], 1, 0)
        out_ref[index] = product * widen_column(jnp.exp(near), one)
        scale_ref[index] = jnp.broadcast_to(widen_column(jnp.exp(far), one), (8, width))


def scan_kernel(me_ref, part_ref, routed_ref, built_ref, out_ref, *, probe_len, heads):
    count, height, width = part_ref.shape
    premise = lax.div(me_ref[0] * height, jnp.int32(DSTATE))
    shape = (DSTATE, width)
    lane = lax.broadcasted_iota(jnp.int32, shape, 0) - premise * heads
    channel = lax.broadcasted_iota(jnp.int32, shape, 1)
    pick = jnp.where(lax.div(channel, jnp.int32(width // heads)) == lane, 1.0, 0.0).astype(BF16)
    state = jnp.zeros((height, width), F32)
    for k in range(count):
        out_ref[k] = state.astype(BF16)
        total = dot(routed_ref[k, probe_len : probe_len + EXTRA, :], pick, 1, 0)
        total = jnp.sum(total[0:8], axis=0, keepdims=True)
        state = state * jnp.exp(total) + part_ref[k].astype(F32)


def apply_kernel(
    table_ref, incoming_ref, routed_ref, local_ref, scale_ref, after_ref, out_ref, done_ref
):
    slots, probe_len, _ = out_ref.shape
    done_ref[...] = jnp.zeros_like(done_ref)
    for slot in range(slots):
        premise = table_ref[4 * slot + 1]
        product = dot(routed_ref[slot, 0:probe_len, :], incoming_ref[premise], 1, 0)
        out_ref[slot] = (product * scale_ref[slot, 0:1, :] + local_ref[slot]).astype(BF16)


def squares(mixed):
    total = mixed[:, 0:128] * mixed[:, 0:128]
    for k in range(1, mixed.shape[1] // 128):
        part = mixed[:, 128 * k : 128 * (k + 1)]
        total = total + part * part
    ones = jnp.ones((8, 128), BF16)
    high, low = pieces(total, 2)
    return dot(ones, high, 1, 1) + dot(ones, low, 1, 1)


def main_kernel(
    in_ref, read_ref, decay_ref, incoming_ref, right_ref, gain_ref, after_ref, out_ref, square_ref
):
    _, length, width = out_ref.shape
    heads = decay_ref.shape[1]
    middle = BLOCK // 2 - 1
    count = length // BLOCK
    one = spread(heads, width)
    twice = spread_twice(one)
    mask = causal(BLOCK, BLOCK)
    line = lax.broadcasted_iota(jnp.int32, (8, BLOCK), 0)
    before = jnp.zeros((heads, 1), F32)
    sums = prefix(decay_ref[0], BLOCK)
    lefts, reaches = [], []
    for k in range(count):
        rows = slice(k * BLOCK, (k + 1) * BLOCK)
        reads = read_ref[0, rows, :]
        gram = jnp.where(mask, dot(reads, in_ref[0, rows, :], 1, 1), 0.0).astype(BF16)
        lefts.append(jnp.concatenate([gram, reads], axis=1))
        mid = sums[k][:, middle : middle + 1]
        reaches.append(widen_column(jnp.exp(before + mid), one))
        before = before + sums[k][:, BLOCK - 1 : BLOCK]
    total = jnp.zeros((8, BLOCK), F32)
    for k in range(count):
        rows = slice(k * BLOCK, (k + 1) * BLOCK)
        product = dot(lefts[k], right_ref[0, k], 1, 0)
        product = product + reaches[k] * dot(read_ref[0, rows, :], incoming_ref[0], 1, 0)
        near = sums[k] - sums[k][:, middle : middle + 1]
        mixed = product * widen(jnp.exp(near), twice)
        out_ref[0, rows, :] = (mixed * gain_ref[...]).astype(BF16)
        total = jnp.where(line == k, squares(mixed), total)
    square_ref[0] = total


def probe_kernel(x_ref, in_ref, read_ref, decay_ref, out_ref, factor_ref, done_ref):
    done_ref[...] = jnp.zeros_like(done_ref)
    probe_dev, length, width = x_ref.shape
    heads = decay_ref.shape[1]
    twice = spread_twice(spread(heads, width))
    mask = causal(length, length)
    for probe in range(probe_dev):
        sums = prefix(decay_ref[probe], length)[0]
        inputs = in_ref[probe]
        scaled = (x_ref[probe].astype(F32) * widen(jnp.exp(-sums), twice)).astype(BF16)
        gram = jnp.where(mask, dot(read_ref[probe], inputs, 1, 1), 0.0).astype(BF16)
        factor = widen(jnp.exp(sums), twice)
        out_ref[probe] = dot(gram, scaled, 1, 0) * factor
        factor_ref[probe] = factor


def join_kernel(
    position_ref, me_ref, inner_ref, factor_ref, gain_ref, arrived_ref, out_ref, square_ref, *, seq_dev
):
    probe_dev, length, width = inner_ref.shape
    pair = 128 // length
    gain = gain_ref[...]
    line = lax.broadcasted_iota(jnp.int32, (8, 128), 0)
    total = jnp.zeros((8, 128), F32)
    for row in range(probe_dev // pair):
        parts = []
        for probe in range(row * pair, (row + 1) * pair):
            owner = lax.div(position_ref[me_ref[0] * probe_dev + probe], jnp.int32(seq_dev))
            parts.append(inner_ref[probe] + factor_ref[probe] * arrived_ref[owner].astype(F32))
        mixed = jnp.concatenate(parts, axis=0)
        out_ref[0, 128 * row : 128 * (row + 1), :] = mixed * gain
        total = jnp.where(line == row, squares(mixed), total)
    for copy in range(square_ref.shape[0]):
        square_ref[copy] = total


def norm_kernel(mixed_ref, *refs):
    out_ref = refs[-1]
    total = 0.0
    for ref in refs[:-1]:
        total = total + jnp.sum(ref[...].reshape(-1, 8, 128), axis=0)
    rate = lax.rsqrt(total / DIN + EPSILON).T
    for k in range(mixed_ref.shape[1] // 128):
        rows = slice(128 * k, 128 * (k + 1))
        out_ref[0, rows, :] = (mixed_ref[0, rows, :].astype(F32) * rate[:, k : k + 1]).astype(BF16)


SMEM = pl.BlockSpec(memory_space=pltpu.SMEM)
VMEM = pl.BlockSpec(memory_space=pltpu.VMEM)
ANY = pl.BlockSpec(memory_space=pl.ANY)


def along(shape, *dims):
    return pl.BlockSpec(
        shape, lambda *at: tuple(at[dims.index(d)] if d in dims else 0 for d in range(len(shape)))
    )


def call(kernel, name, in_specs, out_specs, out_shape, grid=None, scratch=(), limit=58, flops=0, moved=0):
    extra = {} if grid is None else {"grid": grid}
    return pl.pallas_call(
        kernel,
        name=name,
        in_specs=in_specs,
        out_specs=out_specs,
        out_shape=out_shape,
        scratch_shapes=list(scratch),
        compiler_params=pltpu.CompilerParams(vmem_limit_bytes=limit * 1024 * 1024),
        cost_estimate=pl.CostEstimate(flops=flops, bytes_accessed=moved, transcendentals=0),
        **extra,
    )


def shaped(shape, dtype):
    return jax.ShapeDtypeStruct(shape, dtype)


def exchange(value, axis):
    return lax.all_to_all(value, axis, split_axis=0, concat_axis=0, tiled=True)


def local(
    tokens,
    state_inputs,
    state_reads,
    log_decay,
    norm_gain,
    probe_tokens,
    probe_inputs,
    probe_reads,
    probe_decay,
    branch_premise,
    branch_position,
):
    seq = lax.axis_size("seq")
    ring = lax.axis_size("head")
    me = lax.axis_index("seq").astype(jnp.int32).reshape(1)
    row_count, seq_dev, width = tokens.shape
    heads = log_decay.shape[1]
    probe_dev, probe_len, _ = probe_tokens.shape
    height = row_count * DSTATE // seq
    routed_shape = (seq, probe_len + EXTRA, DSTATE)
    count = seq_dev // BLOCK
    depth = BLOCK + DSTATE

    routed, table = call(
        functools.partial(route_kernel, seq_dev=seq_dev),
        "route",
        [SMEM, SMEM, SMEM, along(probe_reads.shape), along(log_decay.shape)],
        [along(routed_shape), SMEM],
        [shaped(routed_shape, BF16), shaped((4 * seq,), jnp.int32)],
        (1,),
        moved=800_000,
    )(branch_position, branch_premise, me, probe_reads, log_decay)
    routed = exchange(routed, "seq")

    x_spec = along((1, seq_dev, width), 0)
    in_spec = along((1, seq_dev, DSTATE), 0)
    decay_spec = along((1, heads, seq_dev), 0)
    ends = call(
        end_kernel,
        "ends",
        [x_spec, in_spec, decay_spec],
        along((1, DSTATE, width), 0),
        shaped((row_count, DSTATE, width), BF16),
        (row_count,),
        [pltpu.VMEM((seq_dev, width), BF16)],
        flops=4_000_000_000,
        moved=20_000_000,
    )(tokens, state_inputs, log_decay)
    parts = exchange(ends.reshape(seq, height, width), "seq")

    token = shaped((8, 128), F32)
    token_spec = pl.BlockSpec((8, 128), lambda *at: (0, 0))
    right, built = call(
        build_kernel,
        "build",
        [x_spec, in_spec, decay_spec],
        [along((1, count, depth, width), 0), token_spec],
        [shaped((row_count, count, depth, width), BF16), token],
        (row_count,),
        flops=5_000_000_000,
        moved=40_000_000,
    )(tokens, state_inputs, log_decay)

    probe_rows = probe_dev * probe_len
    pair = 128 // probe_len
    inner, factor, probed = call(
        probe_kernel,
        "probes",
        [
            along((pair,) + part.shape[1:], 0)
            for part in (probe_tokens, probe_inputs, probe_reads, probe_decay)
        ],
        [along((pair, probe_len, width), 0)] * 2 + [token_spec],
        [shaped(probe_tokens.shape, F32)] * 2 + [token],
        (probe_dev // pair,),
        flops=1_000_000_000,
        moved=8_000_000,
    )(probe_tokens, probe_inputs, probe_reads, probe_decay)

    starts = call(
        functools.partial(scan_kernel, probe_len=probe_len, heads=heads),
        "scan",
        [SMEM, VMEM, along(routed_shape), ANY],
        along((seq, height, width)),
        shaped((seq, height, width), BF16),
        (1,),
        limit=48,
        flops=1_000_000_000,
        moved=2_500_000,
    )(me, parts, routed, built)
    incoming = exchange(starts, "seq").reshape(row_count, DSTATE, width)

    step = 4

    def picked(shape, index, blocked):
        def at(i, t):
            base = 4 * (step * i + index)
            first = (t[base + 1], t[base + 2]) if blocked else (t[base + 1],)
            return first + (0,) * (len(shape) - len(first))

        return pl.BlockSpec(shape, at)

    local_part, scale = pl.pallas_call(
        functools.partial(branch_kernel, step=step),
        name="branch",
        grid_spec=pltpu.PrefetchScalarGridSpec(
            num_scalar_prefetch=1,
            grid=(seq // step,),
            in_specs=[picked((1, 1, depth, width), i, True) for i in range(step)]
            + [picked((1, BLOCK, DSTATE), i, True) for i in range(step)]
            + [picked((1, heads, seq_dev), i, False) for i in range(step)]
            + [along((step,) + routed_shape[1:], 0)],
            out_specs=[along((step, probe_len, width), 0), along((step, 8, width), 0)],
        ),
        out_shape=[shaped((seq, probe_len, width), F32), shaped((seq, 8, width), F32)],
        compiler_params=pltpu.CompilerParams(vmem_limit_bytes=58 * 1024 * 1024),
        cost_estimate=pl.CostEstimate(
            flops=1_000_000_000, bytes_accessed=20_000_000, transcendentals=0
        ),
    )(
        table,
        *[right] * step,
        *[state_inputs] * step,
        *[log_decay] * step,
        routed,
    )

    answers, applied = call(
        apply_kernel,
        "apply",
        [SMEM, VMEM, VMEM, VMEM, VMEM, ANY],
        [along((seq, probe_len, width)), token_spec],
        [shaped((seq, probe_len, width), BF16), token],
        (1,),
        limit=40,
        flops=1_000_000_000,
        moved=8_000_000,
    )(table, incoming, routed, local_part, scale, probed)
    arrived = exchange(answers, "seq")

    gain = norm_gain.reshape(1, width)
    square_spec = along((1, 8, 128), 0)
    square_shape = (row_count, 8, 128)
    mixed, square = call(
        main_kernel,
        "main",
        [
            in_spec,
            in_spec,
            decay_spec,
            along((1, DSTATE, width), 0),
            along((1, count, depth, width), 0),
            along((1, width)),
            ANY,
        ],
        [x_spec, square_spec],
        [shaped(tokens.shape, BF16), shaped(square_shape, F32)],
        (row_count,),
        limit=58,
        flops=12_000_000_000,
        moved=60_000_000,
    )(state_inputs, state_reads, log_decay, incoming, right, gain, applied)
    shared = [square] + [
        lax.ppermute(square, "head", [(i, (i + turn) % ring) for i in range(ring)])
        for turn in range(1, ring)
    ]

    probe_shape = (1, probe_rows, width)
    probe_mixed, probe_square = call(
        functools.partial(join_kernel, seq_dev=seq_dev),
        "join",
        [SMEM, SMEM, VMEM, VMEM, VMEM, VMEM],
        [VMEM, VMEM],
        [shaped(probe_shape, F32), shaped((ring, 8, 128), F32)],
        limit=40,
        flops=1_000_000,
        moved=5_000_000,
    )(branch_position, me, inner, factor, gain, arrived)
    probe_square = exchange(probe_square, "head")

    premise_out = call(
        norm_kernel,
        "norm",
        [x_spec] + [square_spec] * ring,
        x_spec,
        shaped(tokens.shape, BF16),
        (row_count,),
        limit=54,
        flops=1_000_000_000,
        moved=30_000_000,
    )(mixed, *shared)
    probe_out = call(
        norm_kernel,
        "probe_norm",
        [VMEM, VMEM],
        VMEM,
        shaped(probe_shape, BF16),
        limit=40,
        flops=1_000_000,
        moved=2_000_000,
    )(probe_mixed, probe_square)
    return (premise_out, probe_out.reshape(probe_dev, probe_len, width))


def solution(mesh):
    return jax.shard_map(
        local,
        mesh=mesh,
        in_specs=(
            P(None, "seq", "head"),
            P(None, "seq", "head"),
            P(None, "seq", "head"),
            P(None, "head", "seq"),
            P("head"),
            P("seq", None, "head"),
            P("seq", None, "head"),
            P("seq", None, "head"),
            P("seq", "head", None),
            P(),
            P(),
        ),
        out_specs=(P(None, "seq", "head"), P("seq", None, "head")),
        check_vma=False,
    )
```

```python
import functools

import jax
import jax.numpy as jnp
from jax import lax
from jax.experimental import pallas as pl
from jax.experimental.pallas import tpu as pltpu
from jax.sharding import PartitionSpec as P

F32 = jnp.float32
BF16 = jnp.bfloat16
DSTATE = 128
DIN = 8192
EPSILON = 1e-05
BLOCK = 128


def dot(left, right, left_dim, right_dim, precision=None):
    return lax.dot_general(
        left,
        right,
        (((left_dim,), (right_dim,)), ((), ())),
        precision=precision,
        preferred_element_type=F32,
    )


def pieces(value, count):
    parts = []
    for _ in range(count):
        part = value.astype(BF16)
        parts.append(part)
        value = value - part.astype(F32)
    return parts


def spread(heads, width):
    shape = (heads, width)
    head = lax.broadcasted_iota(jnp.int32, shape, 0)
    channel = lax.broadcasted_iota(jnp.int32, shape, 1)
    per_head = width // heads
    return jnp.where(lax.div(channel, jnp.int32(per_head)) == head, 1.0, 0.0).astype(F32)


def spread_twice(one):
    half = one.astype(BF16)
    return jnp.concatenate([half, half], axis=0)


def widen(value, twice):
    return dot(jnp.concatenate(pieces(value, 2), axis=0), twice, 0, 0)


def widen_column(column, one):
    return jnp.sum(column * one, axis=0, keepdims=True)


def prefix(decay, length):
    heads = decay.shape[0]
    count = decay.shape[1] // length
    parts = pieces(decay, 3)
    rows = [part[:, k * length : (k + 1) * length] for k in range(count) for part in parts]
    shape = (length, length)
    upto = (
        lax.broadcasted_iota(jnp.int32, shape, 0) <= lax.broadcasted_iota(jnp.int32, shape, 1)
    )
    total = dot(jnp.concatenate(rows, axis=0), jnp.where(upto, 1.0, 0.0).astype(BF16), 1, 0)
    out = []
    for k in range(count):
        base = 3 * heads * k
        out.append(
            total[base : base + heads]
            + total[base + heads : base + 2 * heads]
            + total[base + 2 * heads : base + 3 * heads]
        )
    return out


def causal(queries, keys):
    shape = (queries, keys)
    return lax.broadcasted_iota(jnp.int32, shape, 0) >= lax.broadcasted_iota(jnp.int32, shape, 1)


def end_kernel(
    position_ref, me_ref, x_ref, in_ref, decay_ref, reads_ref, out_ref, scaled_ref, *, seq_dev, height
):
    _, length, width = x_ref.shape
    heads = decay_ref.shape[1]
    probe_dev, probe_len, _ = reads_ref.shape
    row = pl.program_id(0)
    slices = DSTATE // height
    folds = probe_len // height
    decay = decay_ref[0]
    ones = jnp.ones((height, length), BF16)
    fill = jnp.zeros((DSTATE - heads, length), BF16)
    total = 0.0
    for part in pieces(decay, 3):
        total = total + dot(ones, jnp.concatenate([part, fill], axis=0), 1, 1)
    line = lax.broadcasted_iota(jnp.int32, (height, DSTATE), 0)
    block = jnp.zeros((height, DSTATE), F32)
    for index, part in enumerate(pieces(total, 3)):
        block = jnp.where(line == index, part.astype(F32), block)
    block = block.astype(BF16)
    owners = [
        lax.div(position_ref[me_ref[0] * probe_dev + probe], jnp.int32(seq_dev))
        for probe in range(probe_dev)
    ]
    for part in range(slices):
        rows = slice(part * height, (part + 1) * height)
        chosen = jnp.zeros((probe_len, DSTATE), F32)
        for probe in range(probe_dev):
            here = owners[probe] == row * slices + part
            chosen = jnp.where(here, reads_ref[probe].astype(F32), chosen)
        for fold in range(folds):
            lanes = slice(width + fold * DSTATE, width + (fold + 1) * DSTATE)
            out_ref[0, rows, lanes] = chosen[fold * height : (fold + 1) * height].astype(BF16)
        out_ref[0, rows, width + folds * DSTATE :] = block

    twice = spread_twice(spread(heads, width))
    sums = prefix(decay, BLOCK)
    after = jnp.zeros((heads, 1), F32)
    for k in reversed(range(length // BLOCK)):
        rows = slice(k * BLOCK, (k + 1) * BLOCK)
        last = sums[k][:, BLOCK - 1 : BLOCK]
        factor = widen(jnp.exp((last - sums[k]) + after), twice)
        scaled_ref[rows, :] = (x_ref[0, rows, :].astype(F32) * factor).astype(BF16)
        after = after + last
    out_ref[0, :, 0:width] = dot(in_ref[0], scaled_ref[...], 0, 0).astype(BF16)


def chain_factors(sums, one):
    middle = BLOCK // 2 - 1
    factors = []
    tail = None
    for k in range(len(sums)):
        mid = sums[k][:, middle : middle + 1]
        step = mid if tail is None else tail + mid
        factors.append(widen_column(jnp.exp(step), one))
        tail = sums[k][:, BLOCK - 1 : BLOCK] - mid
    return factors


def build_kernel(
    position_ref, premise_ref, me_ref, x_ref, in_ref, decay_ref, out_ref, table_ref, *, seq_dev, probe_dev
):
    _, length, width = x_ref.shape
    heads = decay_ref.shape[1]
    middle = BLOCK // 2 - 1
    one = spread(heads, width)
    twice = spread_twice(one)
    sums = prefix(decay_ref[0], BLOCK)
    factors = chain_factors(sums, one)
    count = length // BLOCK

    @pl.when(pl.program_id(0) == 0)
    def _():
        me = me_ref[0]
        for slot in range(table_ref.shape[0] // 4):
            offset = jnp.int32(0)
            premise = jnp.int32(0)
            for probe in range(probe_dev):
                position = position_ref[slot * probe_dev + probe]
                here = lax.div(position, jnp.int32(seq_dev)) == me
                offset = jnp.where(here, position - me * seq_dev, offset)
                premise = jnp.where(here, premise_ref[slot * probe_dev + probe], premise)
            block = lax.div(offset, jnp.int32(BLOCK))
            table_ref[4 * slot] = jnp.int32(0)
            table_ref[4 * slot + 1] = premise
            table_ref[4 * slot + 2] = block
            table_ref[4 * slot + 3] = offset - block * BLOCK

    for k in range(count):
        rows = slice(k * BLOCK, (k + 1) * BLOCK)
        near = sums[k] - sums[k][:, middle : middle + 1]
        factor = widen(jnp.exp(-near), twice)
        out_ref[0, k, 0:BLOCK, :] = (x_ref[0, rows, :].astype(F32) * factor).astype(BF16)
    out_ref[0, 0, BLOCK : BLOCK + DSTATE, :] = jnp.zeros((DSTATE, width), BF16)
    written = [
        dot(in_ref[0, k * BLOCK : (k + 1) * BLOCK, :], out_ref[0, k, 0:BLOCK, :], 0, 0)
        for k in range(count - 1)
    ]
    state = written[0]
    for k in range(1, count):
        state = state * factors[k]
        out_ref[0, k, BLOCK : BLOCK + DSTATE, :] = state.astype(BF16)
        if k < count - 1:
            state = state + written[k]


def branch_kernel(table_ref, *refs, step):
    rights, inputs, decays = (refs[i * step : (i + 1) * step] for i in range(3))
    reads_refs, out_ref = refs[3 * step : -1], refs[-1]
    _, depth, width = out_ref.shape
    probe_len = depth - 8
    _, heads, length = decays[0].shape
    one = spread(heads, width)
    lane = lax.broadcasted_iota(jnp.int32, (heads, length), 1)
    key = lax.broadcasted_iota(jnp.int32, (probe_len, BLOCK), 1)
    lefts = []
    for index in range(step):
        slot = pl.program_id(0) * step + index
        reads = jnp.concatenate([ref[index] for ref in reads_refs], axis=0)
        keep = key <= table_ref[4 * slot + 3]
        gram = jnp.where(keep, dot(reads, inputs[index][0], 1, 1), 0.0).astype(BF16)
        lefts.append(jnp.concatenate([gram, reads], axis=1))
    for index in range(step):
        slot = pl.program_id(0) * step + index
        start = table_ref[4 * slot + 2] * BLOCK
        offset = start + table_ref[4 * slot + 3]
        middle = start + BLOCK // 2 - 1
        decay = decays[index][0]
        far = jnp.sum(jnp.where(lane <= offset, decay, 0.0), axis=1, keepdims=True)
        later = jnp.where((lane > middle) & (lane <= offset), decay, 0.0)
        earlier = jnp.where((lane > offset) & (lane <= middle), decay, 0.0)
        near = jnp.sum(later - earlier, axis=1, keepdims=True)
        product = dot(lefts[index], rights[index][0, 0], 1, 0)
        out_ref[index, 0:probe_len, :] = product * widen_column(jnp.exp(near), one)
        scale = widen_column(jnp.exp(far), one)
        out_ref[index, probe_len:, :] = jnp.broadcast_to(scale, (8, width))


def scan_kernel(part_ref, built_ref, probed_ref, out_ref, *, heads):
    count, height, width = out_ref.shape
    shape = (DSTATE, width)
    lane = lax.broadcasted_iota(jnp.int32, shape, 0)
    channel = lax.broadcasted_iota(jnp.int32, shape, 1)
    pick = jnp.where(lax.div(channel, jnp.int32(width // heads)) == lane, 1.0, 0.0).astype(BF16)
    state = jnp.zeros((height, width), F32)
    last = part_ref.shape[2] - DSTATE
    for k in range(count):
        out_ref[k] = state.astype(BF16)
        total = dot(part_ref[k, 0:16, last:], pick, 1, 0)
        total = jnp.sum(total[0:8], axis=0, keepdims=True)
        state = state * jnp.exp(total) + part_ref[k, :, 0:width].astype(F32)


def apply_kernel(table_ref, incoming_ref, *refs):
    reads_refs, local_ref, out_ref = refs[:-2], refs[-2], refs[-1]
    step, probe_len, _ = out_ref.shape
    for index in range(step):
        premise = table_ref[4 * (pl.program_id(0) * step + index) + 1]
        reads = jnp.concatenate([ref[index] for ref in reads_refs], axis=0)
        product = dot(reads, incoming_ref[premise], 1, 0)
        scale = local_ref[index, probe_len : probe_len + 1, :]
        answer = product * scale + local_ref[index, 0:probe_len, :]
        out_ref[index] = answer.astype(BF16)


def squares(mixed):
    half = mixed.astype(BF16)
    return dot(jnp.ones((8, mixed.shape[1]), BF16), half * half, 1, 1)


def main_kernel(
    in_ref, read_ref, decay_ref, incoming_ref, right_ref, gain_ref, out_ref, square_ref
):
    _, length, width = out_ref.shape
    heads = decay_ref.shape[1]
    middle = BLOCK // 2 - 1
    count = length // BLOCK
    one = spread(heads, width)
    twice = spread_twice(one)
    mask = causal(BLOCK, BLOCK)
    line = lax.broadcasted_iota(jnp.int32, (8, BLOCK), 0)
    before = jnp.zeros((heads, 1), F32)
    sums = prefix(decay_ref[0], BLOCK)
    lefts, reaches = [], []
    for k in range(count):
        rows = slice(k * BLOCK, (k + 1) * BLOCK)
        reads = read_ref[0, rows, :]
        gram = jnp.where(mask, dot(reads, in_ref[0, rows, :], 1, 1), 0.0).astype(BF16)
        lefts.append(jnp.concatenate([gram, reads], axis=1))
        mid = sums[k][:, middle : middle + 1]
        reaches.append(widen_column(jnp.exp(before + mid), one))
        before = before + sums[k][:, BLOCK - 1 : BLOCK]
    total = jnp.zeros((8, BLOCK), F32)
    for k in range(count):
        rows = slice(k * BLOCK, (k + 1) * BLOCK)
        product = dot(lefts[k], right_ref[0, k], 1, 0)
        product = product + reaches[k] * dot(read_ref[0, rows, :], incoming_ref[0], 1, 0)
        near = sums[k] - sums[k][:, middle : middle + 1]
        mixed = product * widen(jnp.exp(near), twice)
        out_ref[0, rows, :] = (mixed * gain_ref[...]).astype(BF16)
        total = jnp.where(line == k, squares(mixed), total)
    square_ref[0] = total


def probe_kernel(x_ref, in_ref, read_ref, decay_ref, out_ref, factor_ref, done_ref):
    done_ref[...] = jnp.zeros_like(done_ref)
    probe_dev, length, width = x_ref.shape
    heads = decay_ref.shape[1]
    twice = spread_twice(spread(heads, width))
    mask = causal(length, length)
    for probe in range(probe_dev):
        sums = prefix(decay_ref[probe], length)[0]
        inputs = in_ref[probe]
        scaled = (x_ref[probe].astype(F32) * widen(jnp.exp(-sums), twice)).astype(BF16)
        gram = jnp.where(mask, dot(read_ref[probe], inputs, 1, 1), 0.0).astype(BF16)
        factor = widen(jnp.exp(sums), twice)
        out_ref[probe] = dot(gram, scaled, 1, 0) * factor
        factor_ref[probe] = factor


def join_kernel(
    position_ref, me_ref, inner_ref, factor_ref, gain_ref, arrived_ref, out_ref, square_ref, *, seq_dev
):
    pair, length, width = inner_ref.shape
    row = pl.program_id(0)
    probe_dev = pair * pl.num_programs(0)
    parts = []
    for index in range(pair):
        probe = row * pair + index
        owner = lax.div(position_ref[me_ref[0] * probe_dev + probe], jnp.int32(seq_dev))
        parts.append(inner_ref[index] + factor_ref[index] * arrived_ref[owner].astype(F32))
    mixed = jnp.concatenate(parts, axis=0)
    out_ref[0] = mixed * gain_ref[...]
    total = squares(mixed)
    line = lax.broadcasted_iota(jnp.int32, (8, 128), 0)

    @pl.when(row == 0)
    def _():
        square_ref[...] = jnp.zeros_like(square_ref)

    for copy in range(square_ref.shape[0]):
        square_ref[copy] = jnp.where(line == row, total, square_ref[copy])


def norm_kernel(mixed_ref, *refs):
    out_ref = refs[-1]
    total = 0.0
    for ref in refs[:-1]:
        total = total + jnp.sum(ref[...].reshape((-1,) + (mixed_ref.shape[0], 8, 128)), axis=0)
    for index in range(mixed_ref.shape[0]):
        rate = lax.rsqrt(total[index] / DIN + EPSILON).T
        for k in range(mixed_ref.shape[1] // 128):
            rows = slice(128 * k, 128 * (k + 1))
            scaled = mixed_ref[index, rows, :].astype(F32) * rate[:, k : k + 1]
            out_ref[index, rows, :] = scaled.astype(BF16)


SMEM = pl.BlockSpec(memory_space=pltpu.SMEM)
VMEM = pl.BlockSpec(memory_space=pltpu.VMEM)
ANY = pl.BlockSpec(memory_space=pl.ANY)


def along(shape, *dims):
    return pl.BlockSpec(
        shape, lambda *at: tuple(at[dims.index(d)] if d in dims else 0 for d in range(len(shape)))
    )


def call(kernel, name, in_specs, out_specs, out_shape, grid=None, scratch=(), limit=58, flops=0, moved=0):
    extra = {} if grid is None else {"grid": grid}
    return pl.pallas_call(
        kernel,
        name=name,
        in_specs=in_specs,
        out_specs=out_specs,
        out_shape=out_shape,
        scratch_shapes=list(scratch),
        compiler_params=pltpu.CompilerParams(vmem_limit_bytes=limit * 1024 * 1024),
        cost_estimate=pl.CostEstimate(flops=flops, bytes_accessed=moved, transcendentals=0),
        **extra,
    )


def shaped(shape, dtype):
    return jax.ShapeDtypeStruct(shape, dtype)


def exchange(value, axis):
    return lax.all_to_all(value, axis, split_axis=0, concat_axis=0, tiled=True)


def local(
    tokens,
    state_inputs,
    state_reads,
    log_decay,
    norm_gain,
    probe_tokens,
    probe_inputs,
    probe_reads,
    probe_decay,
    branch_premise,
    branch_position,
):
    seq = lax.axis_size("seq")
    ring = lax.axis_size("head")
    me = lax.axis_index("seq").astype(jnp.int32).reshape(1)
    row_count, seq_dev, width = tokens.shape
    heads = log_decay.shape[1]
    probe_dev, probe_len, _ = probe_tokens.shape
    height = row_count * DSTATE // seq
    count = seq_dev // BLOCK
    depth = BLOCK + DSTATE

    x_spec = along((1, seq_dev, width), 0)
    in_spec = along((1, seq_dev, DSTATE), 0)
    decay_spec = along((1, heads, seq_dev), 0)
    folds = probe_len // height
    wide = width + (folds + 1) * DSTATE
    ends = call(
        functools.partial(end_kernel, seq_dev=seq_dev, height=height),
        "ends",
        [SMEM, SMEM, x_spec, in_spec, decay_spec, along(probe_reads.shape)],
        along((1, DSTATE, wide), 0),
        shaped((row_count, DSTATE, wide), BF16),
        (row_count,),
        [pltpu.VMEM((seq_dev, width), BF16)],
        flops=4_000_000_000,
        moved=20_000_000,
    )(branch_position, me, tokens, state_inputs, log_decay, probe_reads)
    parts = exchange(ends.reshape(seq, height, wide), "seq")

    token = shaped((8, 128), F32)
    token_spec = pl.BlockSpec((8, 128), lambda *at: (0, 0))
    right, table = call(
        functools.partial(build_kernel, seq_dev=seq_dev, probe_dev=probe_dev),
        "build",
        [SMEM, SMEM, SMEM, x_spec, in_spec, decay_spec],
        [along((1, count, depth, width), 0), SMEM],
        [shaped((row_count, count, depth, width), BF16), shaped((4 * seq,), jnp.int32)],
        (row_count,),
        flops=5_000_000_000,
        moved=40_000_000,
    )(branch_position, branch_premise, me, tokens, state_inputs, log_decay)

    probe_rows = probe_dev * probe_len
    pair = 128 // probe_len
    inner, factor, probed = call(
        probe_kernel,
        "probes",
        [
            along((pair,) + part.shape[1:], 0)
            for part in (probe_tokens, probe_inputs, probe_reads, probe_decay)
        ],
        [along((pair, probe_len, width), 0)] * 2 + [token_spec],
        [shaped(probe_tokens.shape, F32)] * 2 + [token],
        (probe_dev // pair,),
        flops=1_000_000_000,
        moved=8_000_000,
    )(probe_tokens, probe_inputs, probe_reads, probe_decay)

    starts = call(
        functools.partial(scan_kernel, heads=heads),
        "scan",
        [VMEM, ANY, ANY],
        along((seq, height, width)),
        shaped((seq, height, width), BF16),
        (1,),
        limit=48,
        flops=1_000_000_000,
        moved=2_500_000,
    )(parts, right, probed)
    incoming = exchange(starts, "seq").reshape(row_count, DSTATE, width)

    step = 4

    def picked(shape, index, blocked):
        def at(i, t):
            base = 4 * (step * i + index)
            first = (t[base + 1], t[base + 2]) if blocked else (t[base + 1],)
            return first + (0,) * (len(shape) - len(first))

        return pl.BlockSpec(shape, at)

    def reads_specs(group):
        first = width // DSTATE
        return [
            pl.BlockSpec((group, height, DSTATE), lambda i, *_, lane=first + fold: (i, 0, lane))
            for fold in range(folds)
        ]

    local_part = pl.pallas_call(
        functools.partial(branch_kernel, step=step),
        name="branch",
        grid_spec=pltpu.PrefetchScalarGridSpec(
            num_scalar_prefetch=1,
            grid=(seq // step,),
            in_specs=[picked((1, 1, depth, width), i, True) for i in range(step)]
            + [picked((1, BLOCK, DSTATE), i, True) for i in range(step)]
            + [picked((1, heads, seq_dev), i, False) for i in range(step)]
            + reads_specs(step),
            out_specs=along((step, probe_len + 8, width), 0),
        ),
        out_shape=shaped((seq, probe_len + 8, width), F32),
        compiler_params=pltpu.CompilerParams(vmem_limit_bytes=58 * 1024 * 1024),
        cost_estimate=pl.CostEstimate(
            flops=1_000_000_000, bytes_accessed=20_000_000, transcendentals=0
        ),
    )(
        table,
        *[right] * step,
        *[state_inputs] * step,
        *[log_decay] * step,
        *[parts] * folds,
    )

    group = seq // 2
    answers = call(
        apply_kernel,
        "apply",
        [SMEM, VMEM] + reads_specs(group) + [along((group, probe_len + 8, width), 0)],
        along((group, probe_len, width), 0),
        shaped((seq, probe_len, width), BF16),
        (seq // group,),
        limit=48,
        flops=1_000_000_000,
        moved=8_000_000,
    )(table, incoming, *[parts] * folds, local_part)
    arrived = exchange(answers, "seq")

    gain = norm_gain.reshape(1, width)
    square_spec = along((1, 8, 128), 0)
    square_shape = (row_count, 8, 128)
    mixed, square = call(
        main_kernel,
        "main",
        [
            in_spec,
            in_spec,
            decay_spec,
            along((1, DSTATE, width), 0),
            along((1, count, depth, width), 0),
            along((1, width)),
        ],
        [x_spec, square_spec],
        [shaped(tokens.shape, BF16), shaped(square_shape, F32)],
        (row_count,),
        limit=58,
        flops=12_000_000_000,
        moved=60_000_000,
    )(state_inputs, state_reads, log_decay, incoming, right, gain)
    shared = [square] + [
        lax.ppermute(square, "head", [(i, (i + turn) % ring) for i in range(ring)])
        for turn in range(1, ring)
    ]

    probe_shape = (1, probe_rows, width)
    probe_mixed, probe_square = call(
        functools.partial(join_kernel, seq_dev=seq_dev),
        "join",
        [
            SMEM,
            SMEM,
            along((pair, probe_len, width), 0),
            along((pair, probe_len, width), 0),
            along((1, width)),
            VMEM,
        ],
        [pl.BlockSpec((1, 128, width), lambda i: (0, i, 0)), along((ring, 8, 128))],
        [shaped(probe_shape, F32), shaped((ring, 8, 128), F32)],
        (probe_dev // pair,),
        limit=52,
        flops=1_000_000,
        moved=5_000_000,
    )(branch_position, me, inner, factor, gain, arrived)
    probe_square = exchange(probe_square, "head")

    premise_out = call(
        norm_kernel,
        "norm",
        [along((2, seq_dev, width), 0)] + [along((2, 8, 128), 0)] * ring,
        along((2, seq_dev, width), 0),
        shaped(tokens.shape, BF16),
        (row_count // 2,),
        limit=54,
        flops=1_000_000_000,
        moved=30_000_000,
    )(mixed, *shared)
    probe_out = call(
        norm_kernel,
        "probe_norm",
        [VMEM, VMEM],
        VMEM,
        shaped(probe_shape, BF16),
        limit=40,
        flops=1_000_000,
        moved=2_000_000,
    )(probe_mixed, probe_square)
    return (premise_out, probe_out.reshape(probe_dev, probe_len, width))


def solution(mesh):
    return jax.shard_map(
        local,
        mesh=mesh,
        in_specs=(
            P(None, "seq", "head"),
            P(None, "seq", "head"),
            P(None, "seq", "head"),
            P(None, "head", "seq"),
            P("head"),
            P("seq", None, "head"),
            P("seq", None, "head"),
            P("seq", None, "head"),
            P("seq", "head", None),
            P(),
            P(),
        ),
        out_specs=(P(None, "seq", "head"), P("seq", None, "head")),
        check_vma=False,
    )
```
